512 devices in a mesh: prow: 64 (over z_lo, x, y), pcol: 8 (over z_hi, core).
Axes of the slice: x: 4, y: 8, z: 8 (z_hi: 4, z_lo: 2; z = z_hi * 2 + z_lo), core: 2. Of those that a mesh axis runs over, the one named last changes fastest.
Arguments:
- ancestor_inverse: float32 [3840, 3840], P('pcol', 'prow'), as said below
- factor: float32 [3840, 16384], P('pcol', 'prow'), may hold values from -0.75 to 0.75
- struct_rows: int32 [64, 11], P('prow'), may hold values from 0 to 14, all different within a row
- diag_factor_inverse: float32 [64, 256, 256], P('prow', 'pcol'), may hold values from -0.375 to 0.375
Outputs:
- selected_inverse: float32 [3840, 16384], P('pcol', 'prow')
- diag_inverse: float32 [64, 256, 256], P('prow', 'pcol')
The draws below stay inside these ranges and needn't reach their ends.
Inputs may be any that keep to these rules, and one draw needn't show every extreme that they name: `struct_rows`: each row lists 11 different ancestor blocks, and every ancestor block is listed by some supernode. ancestor_inverse is symmetric.
All inputs are finite; a program needn't handle non-finite values.
Results may differ from the reference program's by a relative error of at most 0.000073.
Values sent between devices are 32-bit elements; how exact they have to be, the bound alone decides.
A program may use at most 64 MiB of HBM per device.

```python
import math
import jax
import jax.numpy as jnp
from jax import lax

B = 256
R = 15
S = 11
NSUP = 64


def draw_ancestor_inverse(key, part):
    key = jax.random.fold_in(key, 11)
    matrix_order = R * B
    first_key = jax.random.fold_in(key, 0)
    noise = jax.random.normal(first_key, (matrix_order, matrix_order), jnp.float32)
    symmetric = (noise + noise.T) * (0.5 / math.sqrt(matrix_order))
    identity = (jnp.arange(matrix_order)[:, None] == jnp.arange(matrix_order)[None, :]).astype(jnp.float32)
    return symmetric + identity


def level_of(stream_key, extent, cuts, smallest, top_value):
    def one(position, parts):
        heights = jax.random.uniform(jax.random.fold_in(jax.random.fold_in(stream_key, 6), position), (parts,), jnp.float32, smallest / len(cuts), top_value / len(cuts))
        return jnp.repeat(jnp.exp(heights), extent[position] // parts).reshape((-1,) + (1,) * (len(extent) - position - 1))

    loudness = one(*cuts[0])
    for cut in cuts[1:]:
        loudness = loudness * one(*cut)
    return loudness


def choose_distinct(stream_key, rows, count, top, lift):
    sequence = jax.random.permutation(jax.random.fold_in(stream_key, 1), count)
    favour = sequence
    for power in range(3):
        favour = favour * favour // count
    favour = favour * lift // count
    chance = jax.random.randint(jax.random.fold_in(stream_key, 2), (rows, count), 0, 4096) + favour
    fixed_rows = jax.random.permutation(jax.random.fold_in(stream_key, 3), rows)[jnp.arange(count) % rows]
    chance = jnp.where(jnp.arange(rows)[:, None] == fixed_rows[None, :], 1 << 14, chance)
    priority = chance * count + jnp.arange(count)
    return lax.top_k(priority.astype(jnp.int32), top)[1].astype(jnp.int32)


def scatter_about(key, dims, spread, most, pieces=(), kind=jnp.bfloat16):
    result = jax.random.normal(key, dims, jnp.float32) * spread
    if len(pieces) > 0:
        result = level_of(key, dims, pieces, -0.22, 0.18) * result
    return jnp.clip(result, min=-most, max=most).astype(kind)


def setup_inputs(seed: int = 0) -> dict:
    seeds = jax.random.split(jax.random.key(seed), 5)
    return {
        "ancestor_inverse": draw_ancestor_inverse(jax.random.fold_in(seeds[4], 71), 0),
        "factor": scatter_about(seeds[1], (R * B, NSUP * B), 0.125, 0.75, ((0, 8), (1, 64)), jnp.float32),
        "struct_rows": choose_distinct(seeds[2], NSUP, R, S, 6007),
        "diag_factor_inverse": scatter_about(seeds[3], (NSUP, B, B), B ** -0.5, 0.375, ((0, 64), (1, 8)), jnp.float32),
    }


def reference(ancestor_inverse, factor, struct_rows, diag_factor_inverse):
    blocks = jnp.arange(R, dtype=jnp.int32)
    present = jnp.any(struct_rows[:, :, None] == blocks[None, None, :], axis=1)
    keep_mask = present.T.astype(jnp.float32)
    factor_used = factor.reshape(R, B, NSUP, B) * keep_mask[:, None, :, None]
    product = jnp.dot(ancestor_inverse, factor_used.reshape(R * B, NSUP * B), precision=lax.Precision.HIGHEST, preferred_element_type=jnp.float32)
    selected = -(product.reshape(R, B, NSUP, B) * keep_mask[:, None, :, None])
    lower_part = jnp.tril(diag_factor_inverse)
    gram_part = jnp.einsum("kmc,kmd->kcd", lower_part, lower_part, precision=lax.Precision.HIGHEST)
    inner_part = jnp.einsum("jbkc,jbkd->kcd", factor_used, selected, precision=lax.Precision.HIGHEST)
    diag_block = gram_part - inner_part
    return selected.reshape(R * B, NSUP * B), diag_block
```

```python
import jax
import jax.numpy as jnp
import numpy as np
from jax import lax
from jax.experimental import pallas as pl
from jax.experimental.pallas import tpu as pltpu
from jax.sharding import PartitionSpec as P

MESH = pl.DeviceIdType.MESH
F32 = jnp.float32
BF16 = jnp.bfloat16
NX, NY, NZ = 4, 8, 8
B = 256
SLAB = 480
HALF = 240
U0 = 96
U1 = 144


def split(v):
    high = v.astype(BF16)
    return high, (v - high.astype(F32)).astype(BF16)


def dot3(left, right, dims):
    lh, ll = left
    rh, rl = right
    go = lambda p, q: lax.dot_general(p, q, (dims, ((), ())), preferred_element_type=F32)
    return go(lh, rh) + (go(ll, rh) + go(lh, rl))


def kernel(
    a_ref, f_ref, s_ref, d_ref, sel_ref, diag_ref,
    tz, pk, st, ag0, ag1, ah, al, fu, fg, fph, fpl, acc, cr, lb, part, dr,
    send, r_a0, r_x0, r_y1, r_y0, r_x1, r_s0, r_s1, r_f, r_l, r_c, r_d,
):
    def rem(value, by):
        return lax.rem(value, np.int32(by))

    def div(value, by):
        return lax.div(value, np.int32(by))

    r, p = lax.axis_index("prow"), lax.axis_index("pcol")
    a, x, y = div(r, 32), rem(div(r, 8), 4), rem(r, 8)
    zh, c = div(p, 2), rem(p, 2)
    z = 2 * zh + a
    eq, ne = a == c, a != c
    dsg = 1 - 2 * c
    xp, xm, x2 = rem(x + 4 + dsg, 4), rem(x + 4 - dsg, 4), rem(x + 2, 4)

    def yy(k):
        return rem(y + 16 + k * dsg, 8)

    def zz(k):
        return rem(z + 8 + k, 8)

    def dev(x_, y_, z_, c_):
        return (rem(z_, 2) * 32 + x_ * 8 + y_, div(z_, 2) * 2 + c_)

    counter = [0]
    pending = {"all": [], "eq": [], "ne": []}

    def go(src, dst, recv, device, kind="all"):
        copy = pltpu.make_async_remote_copy(
            src_ref=src, dst_ref=dst, send_sem=send.at[counter[0]], recv_sem=recv,
            device_id=device, device_id_type=MESH,
        )
        counter[0] += 1
        copy.start()
        pending[kind].append((src.shape, counter[0] - 1))

    sibling = dev(x, y, z, 1 - c)

    def arrived(dst, recv):
        pltpu.make_async_remote_copy(
            src_ref=dst, dst_ref=dst, send_sem=send.at[0], recv_sem=recv,
            device_id=sibling, device_id_type=MESH,
        ).wait_recv()

    barrier = pltpu.get_barrier_semaphore()
    greeted = [sibling]
    for k in range(1, NZ):
        greeted += [dev(x, y, zz(k), 0), dev(x, y, zz(k), 1)]
    greeted += [dev(xp, y, z, c), dev(xm, y, z, c), dev(x, yy(1), z, c), dev(x, yy(-1), z, c)]
    for device in greeted:
        pl.semaphore_signal(barrier, inc=1, device_id=device, device_id_type=MESH)

    tz[...] = jnp.zeros_like(tz)
    tz[:, 0:60] = a_ref[...]
    for h in range(2):
        pk[h] = tz[HALF * h : HALF * h + 120, :] + pltpu.roll(tz[HALF * h + 120 : HALF * h + 240, :], 64, 1)

    first = div(SLAB * p, B)

    def listed(block):
        total = np.float32(0.0)
        for i in range(s_ref.shape[1]):
            total = jnp.maximum(total, jnp.where(s_ref[0, i] == block, np.float32(1.0), np.float32(0.0)))
        return total

    present = [listed(first + i) for i in range(3)]

    def masked(value):
        block = (lax.broadcasted_iota(jnp.int32, (SLAB, B), 0) + SLAB * p) // B - first
        return value * jnp.where(block == 0, present[0], jnp.where(block == 1, present[1], present[2]))

    fu[...] = masked(f_ref[...])

    @pl.when(eq)
    def _():
        fg[p, 0:SLAB, :] = fu[...]
        st[a] = pk[c]

    for j in range(8):
        fg[j, SLAB : SLAB + 8, :] = jnp.zeros((8, B), F32)
    row = lax.broadcasted_iota(jnp.int32, (32, B), 0) + 32 * p
    lb[0] = jnp.where(row >= lax.broadcasted_iota(jnp.int32, (32, B), 1), d_ref[0], 0.0)
    acc[...] = jnp.zeros_like(acc)

    pl.semaphore_wait(barrier, len(greeted))

    @pl.when(eq)
    def _():
        go(pk.at[1 - c], st.at[a], r_a0.at[a], sibling, "eq")

    @pl.when(ne)
    def _():
        for h in range(2):
            go(pk.at[h], st.at[a], r_a0.at[a], dev(x, y, 2 * zh + c, h), "ne")

    def fslot(j, q):
        return fg.at[j, pl.ds(HALF * q, HALF), :]

    for q in range(2):
        for sign in (1, -1):
            go(fu.at[pl.ds(HALF * q, HALF), :], fslot(p, q), r_f.at[2 * p + q], dev(x, y, zz(sign), a))

    @pl.when(ne)
    def _():
        for q in range(2):
            go(fu.at[pl.ds(HALF * q, HALF), :], fslot(p, q), r_f.at[2 * p + q], sibling, "ne")
        go(lb.at[0], lb.at[1], r_l.at[0], sibling, "ne")

    def f_wait(source, s, q):
        j = 2 * div(source, 2) + s
        arrived(fslot(j, q), r_f.at[2 * j + q])
        return j

    def f_pass(e, distance, sign, kind):
        s, q = e % 2, e // 2
        j = f_wait(zz(-distance * sign), s, q)
        go(fslot(j, q), fslot(j, q), r_f.at[2 * j + q], dev(x, y, zz(sign), c), kind)

    def f1(e):
        @pl.when(ne)
        def _():
            for sign in (1, -1):
                f_pass(e, 1, sign, "ne")

    def f2(e):
        @pl.when(eq)
        def _():
            for sign in (1, -1):
                f_pass(e, 2, sign, "eq")

    def f3(e):
        @pl.when(ne)
        def _():
            s, q = e % 2, e // 2
            way = dsg if e < 3 else -dsg
            j = f_wait(zz(8 - 3 * way), s, q)
            go(fslot(j, q), fslot(j, q), r_f.at[2 * j + q], dev(x, y, zz(way), c), "ne")
            f_wait(zz(3 * way), s, q)

    @pl.when(ne)
    def _():
        arrived(st.at[0], r_a0.at[0])
        arrived(st.at[1], r_a0.at[1])

    @pl.when(eq)
    def _():
        arrived(st.at[1 - a], r_a0.at[1 - a])

    low = lax.broadcasted_iota(jnp.int32, (120, 128), 1) < 64
    p0, p1 = st[0], st[1]
    top = jnp.where(low, p0, pltpu.roll(p1, 64, 1))
    bottom = jnp.where(low, pltpu.roll(p0, 64, 1), p1)
    ag0[c, y, x] = top[0:U0]
    ag1[c, x, y, 0 : 120 - U0, :] = top[U0:120]
    ag1[c, x, y, 120 - U0 : U1, :] = bottom

    yp, ym = yy(1), yy(-1)
    to_xp, to_xm = dev(xp, y, z, c), dev(xm, y, z, c)
    to_yp, to_ym = dev(x, yp, z, c), dev(x, ym, z, c)

    def tile0(x_):
        return ag0.at[c, y, x_]

    def tile1(y_):
        return ag1.at[c, x, y_]

    def bundle0(y_):
        return ag0.at[c, y_]

    def bundle1(x_, half):
        return ag1.at[c, x_, pl.ds(4 * half, 4)]

    def share0(y_):
        go(bundle0(y_), bundle0(y_), r_s0.at[y_], sibling)

    def share1(x_, half):
        go(bundle1(x_, half), bundle1(x_, half), r_s1.at[2 * x_ + half], sibling)

    go(tile0(x), tile0(x), r_x0.at[0], to_xp)
    go(tile0(x), tile0(x), r_x0.at[1], to_xm)
    go(tile1(y), tile1(y), r_y1.at[0], to_yp)
    go(tile1(y), tile1(y), r_y1.at[4], to_ym)

    def y_step(k, part_of, sems, share):
        arrived(part_of(yy(-k)), sems.at[k - 1])
        if k < 4:
            go(part_of(yy(-k)), part_of(yy(-k)), sems.at[k], to_yp)
            arrived(part_of(yy(k)), sems.at[3 + k])
            if k < 3:
                go(part_of(yy(k)), part_of(yy(k)), sems.at[4 + k], to_ym)
        if share is not None:
            share(yy(-k))
            if k < 4:
                share(yy(k))

    arrived(tile0(xm), r_x0.at[0])
    go(tile0(xm), tile0(xm), r_x0.at[2], to_xp)
    y_step(1, tile1, r_y1, None)
    f1(0)
    arrived(tile0(xp), r_x0.at[1])
    arrived(tile0(x2), r_x0.at[2])
    go(bundle0(y), bundle0(y), r_y0.at[0], to_yp)
    go(bundle0(y), bundle0(y), r_y0.at[4], to_ym)
    share0(y)
    y_step(2, tile1, r_y1, None)
    f1(1)
    y_step(3, tile1, r_y1, None)
    f1(2)
    y_step(4, tile1, r_y1, None)
    go(bundle1(x, 0), bundle1(x, 0), r_x1.at[0], to_xp)
    go(bundle1(x, 1), bundle1(x, 1), r_x1.at[2], to_xm)
    go(bundle1(x, 1), bundle1(x, 1), r_x1.at[1], to_xp)
    go(bundle1(x, 0), bundle1(x, 0), r_x1.at[3], to_xm)
    share1(x, 0)
    share1(x, 1)
    y_step(1, bundle0, r_y0, share0)
    f1(3)
    arrived(bundle1(xm, 0), r_x1.at[0])
    go(bundle1(xm, 0), bundle1(xm, 0), r_x1.at[4], to_xp)
    arrived(bundle1(xp, 1), r_x1.at[2])
    go(bundle1(xp, 1), bundle1(xp, 1), r_x1.at[5], to_xm)
    share1(xm, 0)
    share1(xp, 1)
    y_step(2, bundle0, r_y0, share0)

    part[...] = jnp.zeros_like(part)

    @pl.when(eq)
    def _():
        arrived(lb.at[1], r_l.at[0])
        total = jnp.zeros((B, B), F32)
        for i in range(2):
            piece = split(lb[i])
            total = total + dot3(piece, piece, ((0,), (0,)))
        part[...] = total

    f2(0)
    f2(1)
    arrived(bundle1(xm, 1), r_x1.at[1])
    arrived(bundle1(xp, 0), r_x1.at[3])
    share1(xm, 1)
    share1(xp, 0)
    y_step(3, bundle0, r_y0, share0)
    f2(2)
    y_step(4, bundle0, r_y0, share0)
    arrived(bundle1(x2, 0), r_x1.at[4])
    arrived(bundle1(x2, 1), r_x1.at[5])
    share1(x2, 0)
    share1(x2, 1)
    f2(3)

    for k in range(8):
        arrived(ag0.at[1 - c, k], r_s0.at[k])
    for k in range(4):
        for half in range(2):
            arrived(ag1.at[1 - c, k, pl.ds(4 * half, 4)], r_s1.at[2 * k + half])

    def prepare(i):
        xs = div(i, 4)
        m = rem(i, 4)
        lanes = pl.ds(pl.multiple_of(128 * m, 128), 128)
        for h in range(2):
            for ref, at, size in ((ag0, 0, U0), (ag1, U0, U1)):
                if at == 0:
                    t0, t1 = ref[h, 2 * m, xs], ref[h, 2 * m + 1, xs]
                else:
                    t0, t1 = ref[h, xs, 2 * m], ref[h, xs, 2 * m + 1]
                low = lax.broadcasted_iota(jnp.int32, (size, 128), 1) < 64
                for side, value in (
                    (0, jnp.where(low, t0, pltpu.roll(t1, 64, 1))),
                    (4, jnp.where(low, pltpu.roll(t0, 64, 1), t1)),
                ):
                    high, rest = split(value)
                    rows = slice(HALF * h + at, HALF * h + at + size)
                    ah[xs + side, rows, lanes] = high
                    al[xs + side, rows, lanes] = rest

    def prepare_range(lo, hi):
        def body(i, carry):
            prepare(i)
            return carry

        lax.fori_loop(lo, hi, body, 0)

    prepare_range(0, 8)
    f3(0)
    prepare_range(8, 16)
    f3(1)

    def product(t, s):
        near = jnp.where(t == 0, 0, jnp.where(t == 1, -2, jnp.where(t == 2, 2, 4)))
        odd = jnp.where(t == 0, -1, jnp.where(t == 1, 1, jnp.where(t == 2, -3, 3)))
        j = 2 * div(zz(jnp.where(eq, near, odd)), 2) + s
        keep = lax.broadcasted_iota(jnp.int32, (64, B), 0) < 60
        for k in range(8):
            value = jnp.where(keep, fg[j, 60 * k : 60 * k + 64, :], 0.0)
            high, rest = split(value)
            fph[64 * k : 64 * k + 64, :] = high
            fpl[64 * k : 64 * k + 64, :] = rest
        acc[...] += dot3((ah[j], al[j]), (fph[...], fpl[...]), ((1,), (0,)))

    def products(lo, hi):
        def body(i, carry):
            product(div(i, 2), rem(i, 2))
            return carry

        lax.fori_loop(2 * lo, 2 * hi, body, 0)

    @pl.when(eq)
    def _():
        for q in range(2):
            f_wait(z, 1 - c, q)

    products(0, 1)
    f3(2)
    products(1, 2)
    f3(3)
    products(2, 3)

    @pl.when(eq)
    def _():
        for e in range(4):
            f_wait(zz(4), e % 2, e // 2)

    products(3, 4)

    @pl.when(ne)
    def _():
        go(acc, cr, r_c.at[0], dev(x, y, 2 * zh + c, a), "ne")

    part[...] += dot3(split(fg[2 * zh + a, 0:SLAB, :]), split(acc[...]), ((0,), (0,)))

    apart = jnp.where(eq, 0, 1)

    def give(k, core, kind):
        owner = zz(2 * k + apart)
        rows = pl.ds(pl.multiple_of(32 * (2 * div(owner, 2) + core), 32), 32)
        go(part.at[rows, :], dr.at[z], r_d.at[z], dev(x, y, owner, core), kind)

    for k in (2, 1, 3):
        give(k, c, "all")
        give(k, 1 - c, "all")
    give(0, 1 - c, "all")

    @pl.when(ne)
    def _():
        give(0, c, "ne")

    @pl.when(eq)
    def _():
        dr[z] = part[pl.ds(pl.multiple_of(32 * p, 32), 32), :]
        sel_ref[...] = -masked(acc[...])

    @pl.when(ne)
    def _():
        arrived(cr, r_c.at[0])
        sel_ref[...] = -masked(cr[...])
        arrived(dr.at[z], r_d.at[z])

    for k in range(1, 8):
        arrived(dr.at[zz(k)], r_d.at[zz(k)])
    total = dr[0]
    for k in range(1, 8):
        total = total + dr[k]
    diag_ref[0] = total

    def finish(kind):
        like = {
            (HALF, B): fu.at[pl.ds(0, HALF), :],
            (120, 128): pk.at[0],
            (U0, 128): ag0.at[0, 0, 0],
            (U1, 128): ag1.at[0, 0, 0],
            (4, U0, 128): ag0.at[0, 0],
            (4, U1, 128): ag1.at[0, 0, pl.ds(0, 4)],
            (SLAB, B): acc,
            (32, B): lb.at[0],
        }
        for shape, index in pending[kind]:
            pltpu.make_async_remote_copy(
                src_ref=like[shape], dst_ref=like[shape], send_sem=send.at[index], recv_sem=r_l.at[0],
                device_id=sibling, device_id_type=MESH,
            ).wait_send()

    finish("all")

    @pl.when(eq)
    def _():
        finish("eq")

    @pl.when(ne)
    def _():
        finish("ne")


def on_device(ancestor_inverse, factor, struct_rows, diag_factor_inverse):
    vmem = pl.BlockSpec(memory_space=pltpu.VMEM)
    dma = pltpu.SemaphoreType.DMA
    return pl.pallas_call(
        kernel,
        out_shape=(
            jax.ShapeDtypeStruct((SLAB, B), F32),
            jax.ShapeDtypeStruct((1, 32, B), F32),
        ),
        in_specs=[vmem, vmem, pl.BlockSpec(memory_space=pltpu.SMEM), vmem],
        out_specs=(vmem, vmem),
        scratch_shapes=[
            pltpu.VMEM((SLAB, 128), F32),
            pltpu.VMEM((2, 120, 128), F32),
            pltpu.VMEM((2, 120, 128), F32),
            pltpu.VMEM((2, NY, NX, U0, 128), F32),
            pltpu.VMEM((2, NX, NY, U1, 128), F32),
            pltpu.VMEM((8, SLAB, 512), BF16),
            pltpu.VMEM((8, SLAB, 512), BF16),
            pltpu.VMEM((SLAB, B), F32),
            pltpu.VMEM((8, SLAB + 8, B), F32),
            pltpu.VMEM((512, B), BF16),
            pltpu.VMEM((512, B), BF16),
            pltpu.VMEM((SLAB, B), F32),
            pltpu.VMEM((SLAB, B), F32),
            pltpu.VMEM((2, 32, B), F32),
            pltpu.VMEM((B, B), F32),
            pltpu.VMEM((8, 32, B), F32),
            dma((96,)),
            dma((2,)),
            dma((3,)),
            dma((7,)),
            dma((7,)),
            dma((6,)),
            dma((8,)),
            dma((8,)),
            dma((16,)),
            dma((1,)),
            dma((1,)),
            dma((8,)),
        ],
        compiler_params=pltpu.CompilerParams(
            collective_id=0, has_side_effects=True, vmem_limit_bytes=48 * 1024 * 1024
        ),
    )(ancestor_inverse, factor, struct_rows, diag_factor_inverse)


def solution(mesh):
    placed = (P("pcol", "prow"), P("pcol", "prow"), P("prow", None), P("prow", "pcol", None))
    return jax.shard_map(
        on_device,
        mesh=mesh,
        in_specs=placed,
        out_specs=(P("pcol", "prow"), P("prow", "pcol", None)),
        check_vma=False,
    )
```

```python
import jax
import jax.numpy as jnp
import numpy as np
from jax import lax
from jax.experimental import pallas as pl
from jax.experimental.pallas import tpu as pltpu
from jax.sharding import PartitionSpec as P

MESH = pl.DeviceIdType.MESH
F32 = jnp.float32
BF16 = jnp.bfloat16
NX, NY, NZ = 4, 8, 8
B = 256
SLAB = 480
HALF = 240
U0 = 64
U1 = 176
NQ = 4
CHUNK = SLAB // NQ
MOST = 5
EQ_FIRST = (
    ("own",), ("y1", -1), ("y1", 1), ("x0",), ("xp", 1), ("xp", 0), ("y1", -2), ("y1", 2), ("gram",),
    ("y0", 1, -1, 0), ("y0", 1, 1, 0), ("y0", 1, -1, 1), ("y1", -3), ("y0", 2, 1, 0), ("y0", 2, -1, 0),
    ("y0", 1, 1, 1), ("y1", 4), ("y1", 3), ("y0", 2, 1, 1), ("f2", 2, -1), ("y0", 3, -1, 0), ("y0", 3, 1, 0),
    ("xp", 2), ("f2", 0, -1), ("xp", 4), ("f2", 2, 1), ("f2", 0, 1), ("xp", 3), ("f2", 1, -1), ("y0", 2, -1, 1),
    ("sh", 0), ("xp", -1), ("f2", 5, -1), ("y0", 3, 1, 1), ("xp", -2), ("f2", 1, 1), ("xp", -3), ("f2", 4, -1),
    ("f2", 6, 1), ("f2", 4, 1), ("f2", 7, 1), ("f2", 3, 1), ("f2", 3, -1), ("f2", 5, 1), ("sh", 2), ("f2", 6, -1),
    ("sh", 1), ("y0", 3, -1, 1), ("y0", 4, 1, 0), ("f2", 7, -1), ("sh", 3), ("y0", 4, 1, 1),
)
NE_FIRST = (
    ("f1", 0, 1), ("a0",), ("y1", -1), ("x0",), ("f1", 2, 1), ("f1", 1, -1), ("y0", 1, 1, 0), ("y1", 1), ("f1", 3, 1),
    ("f1", 0, -1), ("y1", 2), ("y1", -2), ("f1", 5, 1), ("f1", 1, 1), ("f1", 2, -1), ("y0", 1, -1, 0), ("f1", 5, -1),
    ("f1", 3, -1), ("f1", 6, -1), ("y0", 1, 1, 1), ("y1", 3), ("f1", 7, -1), ("f1", 4, 1), ("y0", 1, -1, 1),
    ("f1", 6, 1), ("y0", 2, 1, 0), ("y1", -3), ("f1", 4, -1), ("y0", 2, -1, 0), ("f1", 7, 1), ("y1", 4), ("xp", 1),
    ("xp", 2), ("y0", 2, 1, 1), ("sh", 0), ("y0", 3, 1, 0), ("xp", 0), ("xp", -1), ("xp", 3), ("xp", -3),
    ("y0", 2, -1, 1), ("xp", -2), ("xp", 4), ("sh", 2), ("y0", 3, 1, 1), ("sh", 1), ("y0", 3, -1, 1),
    ("y0", 3, -1, 0), ("y0", 4, 1, 0), ("f3", 0), ("sh", 3), ("y0", 4, 1, 1), ("f3", 2),
)
NE_LATER = (
    (("f3", 1),),
    (),
    (),
    (("f3", 5), ("f3", 4), ("f3", 7), ("f3", 6), ("f3", 3), ("fr", 0), ("fr", 1), ("fr", 2), ("fr", 3), ("fr", 4), ("fr", 5), ("fr", 6), ("fr", 7)),
)


def split(v):
    high = v.astype(BF16)
    return high, (v - high.astype(F32)).astype(BF16)


def dot3(left, right, dims):
    lh, ll = left
    rh, rl = right
    go = lambda p, q: lax.dot_general(p, q, (dims, ((), ())), preferred_element_type=F32)
    return go(lh, rh) + (go(ll, rh) + go(lh, rl))


def kernel(
    a_ref, f_ref, s_ref, d_ref, sel_ref, diag_ref,
    ta, tw, tz, pk, ag0, ag1, ah, al, fu, fg, fph, fpl, acc, cr, lb, part, pr, dr,
    local, send, r_a0, r_x0, r_y1, r_y0, r_x1, r_s0, r_s1, r_f, r_l, r_c, r_p, r_d,
):
    def rem(value, by):
        return lax.rem(value, np.int32(by))

    def div(value, by):
        return lax.div(value, np.int32(by))

    r, p = lax.axis_index("prow"), lax.axis_index("pcol")
    a, x, y = div(r, 32), rem(div(r, 8), 4), rem(r, 8)
    zh, c = div(p, 2), rem(p, 2)
    z = 2 * zh + a
    eq, ne = a == c, a != c
    dsg = 1 - 2 * c
    xp, xm, x2 = rem(x + 4 + dsg, 4), rem(x + 4 - dsg, 4), rem(x + 2, 4)

    def yy(k):
        return rem(y + 16 + k * dsg, 8)

    def zz(k):
        return rem(z + 8 + k, 8)

    def dev(x_, y_, z_, c_):
        return (rem(z_, 2) * 32 + x_ * 8 + y_, div(z_, 2) * 2 + c_)

    counter = [0]
    pending = {"all": [], "eq": [], "ne": []}

    def go(src, dst, recv, device, kind="all"):
        copy = pltpu.make_async_remote_copy(
            src_ref=src, dst_ref=dst, send_sem=send.at[counter[0]], recv_sem=recv,
            device_id=device, device_id_type=MESH,
        )
        counter[0] += 1
        copy.start()
        pending[kind].append((src.shape, counter[0] - 1))

    sibling = dev(x, y, z, 1 - c)

    def arrived(dst, recv):
        pltpu.make_async_remote_copy(
            src_ref=dst, dst_ref=dst, send_sem=send.at[0], recv_sem=recv,
            device_id=sibling, device_id_type=MESH,
        ).wait_recv()

    loads = [
        pltpu.make_async_copy(a_ref, ta, local.at[0]),
        pltpu.make_async_copy(f_ref, fu, local.at[1]),
        pltpu.make_async_copy(d_ref.at[0], lb.at[0], local.at[2]),
    ]
    for load in loads:
        load.start()
    barrier = pltpu.get_barrier_semaphore()
    greeted = [sibling]
    for k in (1, -1, 2, -2, 4):
        greeted += [dev(x, y, zz(k), 0), dev(x, y, zz(k), 1)]
    greeted += [dev(xp, y, z, c), dev(xm, y, z, c), dev(x2, y, z, c)]
    greeted += [dev(x, yy(k), z, c) for k in (1, -1, 2, -2)]
    for device in greeted:
        pl.semaphore_signal(barrier, inc=1, device_id=device, device_id_type=MESH)

    tw[...] = jnp.zeros_like(tw)
    for load in loads:
        load.wait()
    tw[0:60, 0:SLAB] = ta[...]
    tz[...] = jnp.transpose(tw[...])
    pk[...] = tz[0:HALF, :] + pltpu.roll(tz[HALF:SLAB, :], 64, 1)

    first = div(SLAB * p, B)

    def listed(block):
        total = np.float32(0.0)
        for i in range(s_ref.shape[1]):
            total = jnp.maximum(total, jnp.where(s_ref[0, i] == block, np.float32(1.0), np.float32(0.0)))
        return total

    present = [listed(first + i) for i in range(3)]

    def masked(value):
        block = (lax.broadcasted_iota(jnp.int32, (SLAB, B), 0) + SLAB * p) // B - first
        return value * jnp.where(block == 0, present[0], jnp.where(block == 1, present[1], present[2]))

    fu[...] = masked(fu[...])

    @pl.when(eq)
    def _():
        ag0[c, y, 0] = pk[0:U0, :]
        ag1[c, x, y] = pk[U0:HALF, :]

    row = lax.broadcasted_iota(jnp.int32, (32, B), 0) + 32 * p
    lb[0] = jnp.where(row >= lax.broadcasted_iota(jnp.int32, (32, B), 1), lb[0], 0.0)

    pl.semaphore_wait(barrier, len(greeted))

    @pl.when(ne)
    def _():
        partner = dev(x, y, 2 * zh + c, a)
        go(pk.at[pl.ds(0, U0), :], ag0.at[a, y, 0], r_a0.at[0], partner, "ne")
        go(pk.at[pl.ds(U0, U1), :], ag1.at[a, x, y], r_a0.at[1], partner, "ne")

    def fslot(j, q):
        return fg.at[j, pl.ds(CHUNK * q, CHUNK), :]

    for q in range(NQ):
        for sign in (1, -1):
            go(fu.at[pl.ds(CHUNK * q, CHUNK), :], fslot(p, q), r_f.at[NQ * p + q], dev(x, y, zz(sign), a))

    @pl.when(ne)
    def _():
        for q in range(NQ):
            go(fu.at[pl.ds(CHUNK * q, CHUNK), :], fslot(p, q), r_f.at[NQ * p + q], sibling, "ne")
        go(lb.at[0], lb.at[1], r_l.at[0], sibling, "ne")

    @pl.when(eq)
    def _():
        fg[p, 0:SLAB, :] = fu[...]

    for j in range(8):
        fg[j, SLAB : SLAB + 8, :] = jnp.zeros((8, B), F32)
    acc[...] = jnp.zeros_like(acc)
    part[...] = jnp.zeros_like(part)

    def f_wait(source, s, q):
        j = 2 * div(source, 2) + s
        arrived(fslot(j, q), r_f.at[NQ * j + q])
        return j

    def f_pass(e, distance, sign, kind):
        s, q = e % 2, e // 2
        j = f_wait(zz(-distance * sign), s, q)
        go(fslot(j, q), fslot(j, q), r_f.at[NQ * j + q], dev(x, y, zz(sign), c), kind)

    def f1(e, sign):
        f_pass(e, 1, sign, "ne")

    def f2(e, sign):
        f_pass(e, 2, sign, "eq")

    def f3(e):
        s, q = e % 2, e // 2
        way = dsg if e < MOST else -dsg
        j = f_wait(zz(8 - 3 * way), s, q)
        go(fslot(j, q), fslot(j, q), r_f.at[NQ * j + q], dev(x, y, zz(way), c), "ne")

    def f3_rest(e):
        way = dsg if e < MOST else -dsg
        f_wait(zz(3 * way), e % 2, e // 2)

    to_xp, to_xm, to_x2 = dev(xp, y, z, c), dev(xm, y, z, c), dev(x2, y, z, c)

    def to_y(k):
        return dev(x, yy(k), z, c)

    def tile1(y_):
        return ag1.at[c, x, y_]

    def group0(y_, half):
        return ag0.at[c, y_, pl.ds(3 * half - 2 * half, 1 + 2 * half)]

    def along_x(k):
        src = tile1(yy(k))
        go(src, src, r_x1.at[yy(k)], to_xp, kind[0])
        go(src, src, r_x1.at[8 + yy(k)], to_xm, kind[0])

    def x1_pass(k):
        y_ = yy(k)
        if k in (0, -1, 2, -3):
            src = ag1.at[c, xm, y_]
            arrived(src, r_x1.at[y_])
            go(src, src, r_x1.at[16 + y_], to_xp, kind[0])
        else:
            src = ag1.at[c, xp, y_]
            arrived(src, r_x1.at[8 + y_])
            go(src, src, r_x1.at[16 + y_], to_xm, kind[0])

    def y1_wait(k):
        arrived(tile1(yy(-k)), r_y1.at[k + 3])

    def y1_go(own, k, kind):
        go(tile1(yy(own)), tile1(yy(own)), r_y1.at[k - own + 3], to_y(k), kind)

    def y0_go(k, sign, half):
        src = group0(yy(-sign * (k - 1)), half)
        go(src, src, r_y0.at[2 * (k - 1 + (0 if sign > 0 else 4)) + half], to_y(sign), kind[0])

    kind = ["all"]
    seen = set()

    def share0(y_):
        src = ag0.at[c, y_]
        go(src, src, r_s0.at[y_], sibling, kind[0])

    def share1(x_):
        src = ag1.at[c, x_]
        go(src, src, r_s1.at[x_], sibling, kind[0])

    def own_out():
        for k in (1, -1, 2, -2):
            y1_go(0, k, kind[0])
        src = ag0.at[c, y, 0]
        go(src, ag0.at[c, y, 2 + dsg], r_x0.at[0], to_xp, kind[0])
        go(src, ag0.at[c, y, 2 - dsg], r_x0.at[1], to_xm, kind[0])
        go(src, ag0.at[c, y, 2], r_x0.at[2], to_x2, kind[0])
        along_x(0)
        for sign in (1, -1):
            y0_go(1, sign, 0)

    def do_a0():
        arrived(ag0.at[c, y, 0], r_a0.at[0])
        arrived(ag1.at[c, x, y], r_a0.at[1])
        own_out()

    def do_x0():
        arrived(ag0.at[c, y, 2 + dsg], r_x0.at[0])
        arrived(ag0.at[c, y, 2 - dsg], r_x0.at[1])
        arrived(ag0.at[c, y, 2], r_x0.at[2])
        for sign in (1, -1):
            y0_go(1, sign, 1)
        share0(y)

    def do_y1(k):
        y1_wait(k)
        if k == 2:
            y1_go(-2, 1, kind[0])
            y1_go(-2, 2, kind[0])
        if k == -2:
            y1_go(2, -1, kind[0])
        along_x(4 if k == 4 else -k)

    def do_y0(k, sign, half):
        arrived(group0(yy(-sign * k), half), r_y0.at[2 * (k - 1 + (0 if sign > 0 else 4)) + half])
        if k < (4 if sign > 0 else 3):
            y0_go(k + 1, sign, half)
        if (k, sign) in seen:
            share0(yy(-sign * k))
        seen.add((k, sign))

    FROM_M = (0, -1, 2, -3)
    TILES = (0, 1, -1, 2, -2, 3, -3, 4)

    def do_share(which):
        if which == 0:
            share1(x)
        elif which == 1:
            for k in TILES:
                if k not in FROM_M:
                    arrived(ag1.at[c, xm, yy(k)], r_x1.at[yy(k)])
            share1(xm)
        elif which == 2:
            for k in TILES:
                if k in FROM_M:
                    arrived(ag1.at[c, xp, yy(k)], r_x1.at[8 + yy(k)])
            share1(xp)
        else:
            for k in TILES:
                arrived(ag1.at[c, x2, yy(k)], r_x1.at[16 + yy(k)])
            share1(x2)

    def gram():
        arrived(lb.at[1], r_l.at[0])
        total = jnp.zeros((B, B), F32)
        for i in range(2):
            piece = split(lb[i])
            total = total + dot3(piece, piece, ((0,), (0,)))
        part[...] = total

    steps = {
        "own": own_out, "a0": do_a0, "x0": do_x0, "y1": do_y1, "y0": do_y0, "xp": x1_pass, "sh": do_share,
        "f1": f1, "f2": f2, "f3": f3, "fr": f3_rest, "gram": gram,
    }

    def run(which, order):
        kind[0] = which
        seen.clear()
        for step in order:
            steps[step[0]](*step[1:])

    def both(order_eq, order_ne):
        @pl.when(eq)
        def _():
            run("eq", order_eq)

        @pl.when(ne)
        def _():
            run("ne", order_ne)

    both(EQ_FIRST, NE_FIRST)

    for k in range(8):
        arrived(ag0.at[1 - c, k], r_s0.at[k])
    for k in range(4):
        arrived(ag1.at[1 - c, k], r_s1.at[k])

    def prepare(i):
        xs = div(i, 4)
        m = rem(i, 4)
        lanes = pl.ds(pl.multiple_of(128 * m, 128), 128)
        for side in range(2):
            for ref, at, size in ((ag0, 0, U0), (ag1, U0, U1)):
                if ref is ag0:
                    t0, t1 = ref[side, 2 * m, rem(xs - x + 4, 4)], ref[side, 2 * m + 1, rem(xs - x + 4, 4)]
                else:
                    t0, t1 = ref[side, xs, 2 * m], ref[side, xs, 2 * m + 1]
                low = lax.broadcasted_iota(jnp.int32, (size, 128), 1) < 64
                for top, value in (
                    (at, jnp.where(low, t0, pltpu.roll(t1, 64, 1))),
                    (HALF + at, jnp.where(low, pltpu.roll(t0, 64, 1), t1)),
                ):
                    high, rest = split(value)
                    ah[xs + 4 * side, top : top + size, lanes] = high
                    al[xs + 4 * side, top : top + size, lanes] = rest

    def prepare_range(lo, hi):
        def body(i, carry):
            prepare(i)
            return carry

        lax.fori_loop(lo, hi, body, 0)

    prepare_range(0, 8)
    both((), NE_LATER[0])
    prepare_range(8, 16)
    both((), NE_LATER[1])

    def product(t, s):
        near = jnp.where(t == 0, 0, jnp.where(t == 1, -2, jnp.where(t == 2, 2, 4)))
        odd = jnp.where(t == 0, -1, jnp.where(t == 1, 1, jnp.where(t == 2, -3, 3)))
        j = 2 * div(zz(jnp.where(eq, near, odd)), 2) + s
        keep = lax.broadcasted_iota(jnp.int32, (64, B), 0) < 60
        for k in range(8):
            value = jnp.where(keep, fg[j, 60 * k : 60 * k + 64, :], 0.0)
            high, rest = split(value)
            fph[64 * k : 64 * k + 64, :] = high
            fpl[64 * k : 64 * k + 64, :] = rest
        acc[...] += dot3((ah[j], al[j]), (fph[...], fpl[...]), ((1,), (0,)))

    def products(lo, hi):
        def body(i, carry):
            product(div(i, 2), rem(i, 2))
            return carry

        lax.fori_loop(lo, hi, body, 0)

    @pl.when(eq)
    def _():
        for q in range(NQ):
            f_wait(z, 1 - c, q)

    products(0, 2)
    both((), NE_LATER[2])
    products(2, 4)
    both((), NE_LATER[3])
    products(4, 6)
    for s in range(2):
        @pl.when(eq)
        def _():
            for q in range(NQ):
                f_wait(zz(4), s, q)

        products(6 + s, 7 + s)

    @pl.when(ne)
    def _():
        go(acc, cr, r_c.at[0], dev(x, y, 2 * zh + c, a), "ne")

    part[...] += dot3(split(fg[2 * zh + a, 0:SLAB, :]), split(acc[...]), ((0,), (0,)))

    @pl.when(ne)
    def _():
        go(part, pr, r_p.at[0], dev(x, y, zz(2 * a - 1), c), "ne")

    def give(k, core):
        owner = zz(2 * k)
        rows = pl.ds(pl.multiple_of(32 * (2 * div(owner, 2) + core), 32), 32)
        go(part.at[rows, :], dr.at[zh], r_d.at[zh], dev(x, y, owner, core), "eq")

    @pl.when(eq)
    def _():
        arrived(pr, r_p.at[0])
        part[...] += pr[...]
        for k in (2, 1, 3):
            give(k, c)
            give(k, 1 - c)
        give(0, 1 - c)

    @pl.when(eq)
    def _():
        dr[zh] = part[pl.ds(pl.multiple_of(32 * p, 32), 32), :]
        sel_ref[...] = -masked(acc[...])

    @pl.when(ne)
    def _():
        arrived(cr, r_c.at[0])
        sel_ref[...] = -masked(cr[...])
        arrived(dr.at[zh], r_d.at[zh])

    for k in range(1, 4):
        arrived(dr.at[rem(zh + k, 4)], r_d.at[rem(zh + k, 4)])
    total = dr[0]
    for k in range(1, 4):
        total = total + dr[k]
    diag_ref[0] = total

    def finish(kind):
        like = {
            (CHUNK, B): fu.at[pl.ds(0, CHUNK), :],
            (U0, 128): ag0.at[0, 0, 0],
            (U1, 128): ag1.at[0, 0, 0],
            (1, U0, 128): ag0.at[0, 0, pl.ds(0, 1)],
            (3, U0, 128): ag0.at[0, 0, pl.ds(0, 3)],
            (B, B): part,
            (4, U0, 128): ag0.at[0, 0],
            (8, U1, 128): ag1.at[0, 0],
            (SLAB, B): acc,
            (32, B): lb.at[0],
        }
        for shape, index in pending[kind]:
            pltpu.make_async_remote_copy(
                src_ref=like[shape], dst_ref=like[shape], send_sem=send.at[index], recv_sem=r_l.at[0],
                device_id=sibling, device_id_type=MESH,
            ).wait_send()

    finish("all")

    @pl.when(eq)
    def _():
        finish("eq")

    @pl.when(ne)
    def _():
        finish("ne")


def on_device(ancestor_inverse, factor, struct_rows, diag_factor_inverse):
    vmem = pl.BlockSpec(memory_space=pltpu.VMEM)
    anywhere = pl.BlockSpec(memory_space=pl.ANY)
    dma = pltpu.SemaphoreType.DMA
    return pl.pallas_call(
        kernel,
        out_shape=(
            jax.ShapeDtypeStruct((SLAB, B), F32),
            jax.ShapeDtypeStruct((1, 32, B), F32),
        ),
        in_specs=[anywhere, anywhere, pl.BlockSpec(memory_space=pltpu.SMEM), anywhere],
        out_specs=(vmem, vmem),
        scratch_shapes=[
            pltpu.VMEM((60, SLAB), F32),
            pltpu.VMEM((128, 512), F32),
            pltpu.VMEM((512, 128), F32),
            pltpu.VMEM((HALF, 128), F32),
            pltpu.VMEM((2, NY, NX, U0, 128), F32),
            pltpu.VMEM((2, NX, NY, U1, 128), F32),
            pltpu.VMEM((8, SLAB, 512), BF16),
            pltpu.VMEM((8, SLAB, 512), BF16),
            pltpu.VMEM((SLAB, B), F32),
            pltpu.VMEM((8, SLAB + 8, B), F32),
            pltpu.VMEM((512, B), BF16),
            pltpu.VMEM((512, B), BF16),
            pltpu.VMEM((SLAB, B), F32),
            pltpu.VMEM((SLAB, B), F32),
            pltpu.VMEM((2, 32, B), F32),
            pltpu.VMEM((B, B), F32),
            pltpu.VMEM((B, B), F32),
            pltpu.VMEM((4, 32, B), F32),
            dma((3,)),
            dma((256,)),
            dma((2,)),
            dma((3,)),
            dma((8,)),
            dma((14,)),
            dma((24,)),
            dma((8,)),
            dma((4,)),
            dma((8 * NQ,)),
            dma((1,)),
            dma((1,)),
            dma((1,)),
            dma((4,)),
        ],
        compiler_params=pltpu.CompilerParams(
            collective_id=0, has_side_effects=True, vmem_limit_bytes=60 * 1024 * 1024
        ),
    )(ancestor_inverse.T, factor, struct_rows, diag_factor_inverse)


def solution(mesh):
    placed = (P("pcol", "prow"), P("pcol", "prow"), P("prow", None), P("prow", "pcol", None))
    return jax.shard_map(
        on_device,
        mesh=mesh,
        in_specs=placed,
        out_specs=(P("pcol", "prow"), P("prow", "pcol", None)),
        check_vma=False,
    )
```

```python
import jax
import jax.numpy as jnp
import numpy as np
from jax import lax
from jax.experimental import pallas as pl
from jax.experimental.pallas import tpu as pltpu
from jax.sharding import PartitionSpec as P

MESH = pl.DeviceIdType.MESH
F32 = jnp.float32
BF16 = jnp.bfloat16
NX, NY, NZ = 4, 8, 8
B = 256
SLAB = 480
HALF = 240
U0 = 64
U1 = 176
NQ = 4
CHUNK = SLAB // NQ
MOST = 5
EQ_FIRST = (
    ("own",), ("y1", -1), ("y1", 1), ("x0",), ("xp", 1), ("xp", 0), ("y1", -2), ("y1", 2), ("gram",),
    ("y0", 1, -1, 0), ("y0", 1, 1, 0), ("y0", 1, -1, 1), ("y1", -3), ("y0", 2, 1, 0), ("y0", 2, -1, 0),
    ("y0", 1, 1, 1), ("y1", 4), ("y1", 3), ("y0", 2, 1, 1), ("f2", 2, -1), ("y0", 3, -1, 0), ("y0", 3, 1, 0),
    ("xp", 2), ("f2", 0, -1), ("xp", 4), ("f2", 2, 1), ("f2", 0, 1), ("xp", 3), ("f2", 1, -1), ("y0", 2, -1, 1),
    ("sh", 0), ("xp", -1), ("f2", 5, -1), ("y0", 3, 1, 1), ("xp", -2), ("f2", 1, 1), ("xp", -3), ("f2", 4, -1),
    ("f2", 6, 1), ("f2", 4, 1), ("f2", 7, 1), ("f2", 3, 1), ("f2", 3, -1), ("f2", 5, 1), ("sh", 2), ("f2", 6, -1),
    ("sh", 1), ("y0", 3, -1, 1), ("y0", 4, 1, 0), ("f2", 7, -1), ("sh", 3), ("y0", 4, 1, 1),
)
NE_FIRST = (
    ("f1", 0, 1), ("a0",), ("y1", -1), ("x0",), ("f1", 2, 1), ("f1", 1, -1), ("y0", 1, 1, 0), ("y1", 1), ("f1", 3, 1),
    ("f1", 0, -1), ("y1", 2), ("y1", -2), ("f1", 5, 1), ("f1", 1, 1), ("f1", 2, -1), ("y0", 1, -1, 0), ("f1", 5, -1),
    ("f1", 3, -1), ("f1", 6, -1), ("y0", 1, 1, 1), ("y1", 3), ("f1", 7, -1), ("f1", 4, 1), ("y0", 1, -1, 1),
    ("f1", 6, 1), ("y0", 2, 1, 0), ("y1", -3), ("f1", 4, -1), ("y0", 2, -1, 0), ("f1", 7, 1), ("y1", 4), ("xp", 1),
    ("xp", 2), ("y0", 2, 1, 1), ("sh", 0), ("y0", 3, 1, 0), ("xp", 0), ("xp", -1), ("xp", 3), ("xp", -3),
    ("y0", 2, -1, 1), ("xp", -2), ("xp", 4), ("sh", 2), ("y0", 3, 1, 1), ("sh", 1), ("y0", 3, -1, 1),
    ("y0", 3, -1, 0), ("y0", 4, 1, 0), ("f3", 0), ("sh", 3), ("y0", 4, 1, 1), ("f3", 2),
)
NE_LATER = (
    (("f3", 1),),
    (),
    (),
    (("f3", 5), ("f3", 4), ("f3", 7), ("f3", 6), ("f3", 3), ("fr", 0), ("fr", 1), ("fr", 2), ("fr", 3), ("fr", 4), ("fr", 5), ("fr", 6), ("fr", 7)),
)


def split(v):
    high = v.astype(BF16)
    return high, (v - high.astype(F32)).astype(BF16)


def dot3(left, right, dims):
    lh, ll = left
    rh, rl = right
    go = lambda p, q: lax.dot_general(p, q, (dims, ((), ())), preferred_element_type=F32)
    return go(lh, rh) + (go(ll, rh) + go(lh, rl))


def kernel(
    a_ref, f_ref, s_ref, d_ref, sel_ref, diag_ref,
    sel_v, diag_v, ta, tw, tz, pk, ag0, ag1, ah, al, fu, fg, fph, fpl, acc, cr, lb, part, pr, dr,
    local, send, r_a0, r_x0, r_y1, r_y0, r_x1, r_s0, r_s1, r_f, r_l, r_c, r_p, r_d,
):
    def rem(value, by):
        return lax.rem(value, np.int32(by))

    def div(value, by):
        return lax.div(value, np.int32(by))

    r, p = lax.axis_index("prow"), lax.axis_index("pcol")
    a, x, y = div(r, 32), rem(div(r, 8), 4), rem(r, 8)
    zh, c = div(p, 2), rem(p, 2)
    z = 2 * zh + a
    eq, ne = a == c, a != c
    dsg = 1 - 2 * c
    xp, xm, x2 = rem(x + 4 + dsg, 4), rem(x + 4 - dsg, 4), rem(x + 2, 4)

    def yy(k):
        return rem(y + 16 + k * dsg, 8)

    def zz(k):
        return rem(z + 8 + k, 8)

    def dev(x_, y_, z_, c_):
        return (rem(z_, 2) * 32 + x_ * 8 + y_, div(z_, 2) * 2 + c_)

    counter = [0]
    pending = {"all": [], "eq": [], "ne": []}

    def go(src, dst, recv, device, kind="all"):
        copy = pltpu.make_async_remote_copy(
            src_ref=src, dst_ref=dst, send_sem=send.at[counter[0]], recv_sem=recv,
            device_id=device, device_id_type=MESH,
        )
        counter[0] += 1
        copy.start()
        pending[kind].append((src.shape, counter[0] - 1))

    sibling = dev(x, y, z, 1 - c)

    def arrived(dst, recv):
        pltpu.make_async_remote_copy(
            src_ref=dst, dst_ref=dst, send_sem=send.at[0], recv_sem=recv,
            device_id=sibling, device_id_type=MESH,
        ).wait_recv()

    loads = [
        pltpu.make_async_copy(a_ref, ta, local.at[0]),
        pltpu.make_async_copy(f_ref, fu, local.at[1]),
        pltpu.make_async_copy(d_ref.at[0], lb.at[0], local.at[2]),
    ]
    for load in loads:
        load.start()
    barrier = pltpu.get_barrier_semaphore()
    greeted = [sibling]
    for k in (1, -1):
        greeted += [dev(x, y, zz(k), 0), dev(x, y, zz(k), 1)]
    greeted += [dev(xp, y, z, c), dev(xm, y, z, c), dev(x2, y, z, c)]
    greeted += [dev(x, yy(k), z, c) for k in (1, -1, 2, -2)]
    for device in greeted:
        pl.semaphore_signal(barrier, inc=1, device_id=device, device_id_type=MESH)

    tw[...] = jnp.zeros_like(tw)
    for load in loads:
        load.wait()
    tw[0:60, 0:SLAB] = ta[...]
    tz[...] = jnp.transpose(tw[...])
    pk[...] = tz[0:HALF, :] + pltpu.roll(tz[HALF:SLAB, :], 64, 1)

    first = div(SLAB * p, B)

    def listed(block):
        total = np.float32(0.0)
        for i in range(s_ref.shape[1]):
            total = jnp.maximum(total, jnp.where(s_ref[0, i] == block, np.float32(1.0), np.float32(0.0)))
        return total

    present = [listed(first + i) for i in range(3)]

    def masked(value):
        block = (lax.broadcasted_iota(jnp.int32, (SLAB, B), 0) + SLAB * p) // B - first
        return value * jnp.where(block == 0, present[0], jnp.where(block == 1, present[1], present[2]))

    fu[...] = masked(fu[...])

    @pl.when(eq)
    def _():
        ag0[c, y, 0] = pk[0:U0, :]
        ag1[c, x, y] = pk[U0:HALF, :]

    row = lax.broadcasted_iota(jnp.int32, (32, B), 0) + 32 * p
    lb[0] = jnp.where(row >= lax.broadcasted_iota(jnp.int32, (32, B), 1), lb[0], 0.0)

    pl.semaphore_wait(barrier, len(greeted))

    @pl.when(ne)
    def _():
        partner = dev(x, y, 2 * zh + c, a)
        go(pk.at[pl.ds(0, U0), :], ag0.at[a, y, 0], r_a0.at[0], partner, "ne")
        go(pk.at[pl.ds(U0, U1), :], ag1.at[a, x, y], r_a0.at[1], partner, "ne")

    def fslot(j, q):
        return fg.at[j, pl.ds(CHUNK * q, CHUNK), :]

    for q in range(NQ):
        for sign in (1, -1):
            go(fu.at[pl.ds(CHUNK * q, CHUNK), :], fslot(p, q), r_f.at[NQ * p + q], dev(x, y, zz(sign), a))

    @pl.when(ne)
    def _():
        for q in range(NQ):
            go(fu.at[pl.ds(CHUNK * q, CHUNK), :], fslot(p, q), r_f.at[NQ * p + q], sibling, "ne")
        go(lb.at[0], lb.at[1], r_l.at[0], sibling, "ne")

    @pl.when(eq)
    def _():
        fg[p, 0:SLAB, :] = fu[...]

    for j in range(8):
        fg[j, SLAB : SLAB + 8, :] = jnp.zeros((8, B), F32)
    acc[...] = jnp.zeros_like(acc)
    part[...] = jnp.zeros_like(part)

    def f_wait(source, s, q):
        j = 2 * div(source, 2) + s
        arrived(fslot(j, q), r_f.at[NQ * j + q])
        return j

    def f_pass(e, distance, sign, kind):
        s, q = e % 2, e // 2
        j = f_wait(zz(-distance * sign), s, q)
        go(fslot(j, q), fslot(j, q), r_f.at[NQ * j + q], dev(x, y, zz(sign), c), kind)

    def f1(e, sign):
        f_pass(e, 1, sign, "ne")

    def f2(e, sign):
        f_pass(e, 2, sign, "eq")

    def f3(e):
        s, q = e % 2, e // 2
        way = dsg if e < MOST else -dsg
        j = f_wait(zz(8 - 3 * way), s, q)
        go(fslot(j, q), fslot(j, q), r_f.at[NQ * j + q], dev(x, y, zz(way), c), "ne")

    def f3_rest(e):
        way = dsg if e < MOST else -dsg
        f_wait(zz(3 * way), e % 2, e // 2)

    to_xp, to_xm, to_x2 = dev(xp, y, z, c), dev(xm, y, z, c), dev(x2, y, z, c)

    def to_y(k):
        return dev(x, yy(k), z, c)

    def tile1(y_):
        return ag1.at[c, x, y_]

    def group0(y_, half):
        return ag0.at[c, y_, pl.ds(3 * half - 2 * half, 1 + 2 * half)]

    def along_x(k):
        src = tile1(yy(k))
        go(src, src, r_x1.at[yy(k)], to_xp, kind[0])
        go(src, src, r_x1.at[8 + yy(k)], to_xm, kind[0])

    def x1_pass(k):
        y_ = yy(k)
        if k in (0, -1, 2, -3):
            src = ag1.at[c, xm, y_]
            arrived(src, r_x1.at[y_])
            go(src, src, r_x1.at[16 + y_], to_xp, kind[0])
        else:
            src = ag1.at[c, xp, y_]
            arrived(src, r_x1.at[8 + y_])
            go(src, src, r_x1.at[16 + y_], to_xm, kind[0])

    def y1_wait(k):
        arrived(tile1(yy(-k)), r_y1.at[k + 3])

    def y1_go(own, k, kind):
        go(tile1(yy(own)), tile1(yy(own)), r_y1.at[k - own + 3], to_y(k), kind)

    def y0_go(k, sign, half):
        src = group0(yy(-sign * (k - 1)), half)
        go(src, src, r_y0.at[2 * (k - 1 + (0 if sign > 0 else 4)) + half], to_y(sign), kind[0])

    kind = ["all"]
    seen = set()

    def share0(y_):
        src = ag0.at[c, y_]
        go(src, src, r_s0.at[y_], sibling, kind[0])

    def share1(x_):
        src = ag1.at[c, x_]
        go(src, src, r_s1.at[x_], sibling, kind[0])

    def own_out():
        for k in (1, -1, 2, -2):
            y1_go(0, k, kind[0])
        src = ag0.at[c, y, 0]
        go(src, ag0.at[c, y, 2 + dsg], r_x0.at[0], to_xp, kind[0])
        go(src, ag0.at[c, y, 2 - dsg], r_x0.at[1], to_xm, kind[0])
        go(src, ag0.at[c, y, 2], r_x0.at[2], to_x2, kind[0])
        along_x(0)
        for sign in (1, -1):
            y0_go(1, sign, 0)

    def do_a0():
        arrived(ag0.at[c, y, 0], r_a0.at[0])
        arrived(ag1.at[c, x, y], r_a0.at[1])
        own_out()

    def do_x0():
        arrived(ag0.at[c, y, 2 + dsg], r_x0.at[0])
        arrived(ag0.at[c, y, 2 - dsg], r_x0.at[1])
        arrived(ag0.at[c, y, 2], r_x0.at[2])
        for sign in (1, -1):
            y0_go(1, sign, 1)
        share0(y)

    def do_y1(k):
        y1_wait(k)
        if k == 2:
            y1_go(-2, 1, kind[0])
            y1_go(-2, 2, kind[0])
        if k == -2:
            y1_go(2, -1, kind[0])
        along_x(4 if k == 4 else -k)

    def do_y0(k, sign, half):
        arrived(group0(yy(-sign * k), half), r_y0.at[2 * (k - 1 + (0 if sign > 0 else 4)) + half])
        if k < (4 if sign > 0 else 3):
            y0_go(k + 1, sign, half)
        if (k, sign) in seen:
            share0(yy(-sign * k))
        seen.add((k, sign))

    FROM_M = (0, -1, 2, -3)
    TILES = (0, 1, -1, 2, -2, 3, -3, 4)

    def do_share(which):
        if which == 0:
            share1(x)
        elif which == 1:
            for k in TILES:
                if k not in FROM_M:
                    arrived(ag1.at[c, xm, yy(k)], r_x1.at[yy(k)])
            share1(xm)
        elif which == 2:
            for k in TILES:
                if k in FROM_M:
                    arrived(ag1.at[c, xp, yy(k)], r_x1.at[8 + yy(k)])
            share1(xp)
        else:
            for k in TILES:
                arrived(ag1.at[c, x2, yy(k)], r_x1.at[16 + yy(k)])
            share1(x2)

    def gram():
        arrived(lb.at[1], r_l.at[0])
        total = jnp.zeros((B, B), F32)
        for i in range(2):
            piece = split(lb[i])
            total = total + dot3(piece, piece, ((0,), (0,)))
        part[...] = total

    steps = {
        "own": own_out, "a0": do_a0, "x0": do_x0, "y1": do_y1, "y0": do_y0, "xp": x1_pass, "sh": do_share,
        "f1": f1, "f2": f2, "f3": f3, "fr": f3_rest, "gram": gram,
    }

    def run(which, order):
        kind[0] = which
        seen.clear()
        for step in order:
            steps[step[0]](*step[1:])

    def both(order_eq, order_ne):
        @pl.when(eq)
        def _():
            run("eq", order_eq)

        @pl.when(ne)
        def _():
            run("ne", order_ne)

    both(EQ_FIRST, NE_FIRST)

    for k in range(8):
        arrived(ag0.at[1 - c, k], r_s0.at[k])
    for k in range(4):
        arrived(ag1.at[1 - c, k], r_s1.at[k])

    def prepare(i):
        xs = div(i, 4)
        m = rem(i, 4)
        lanes = pl.ds(pl.multiple_of(128 * m, 128), 128)
        for side in range(2):
            for ref, at, size in ((ag0, 0, U0), (ag1, U0, U1)):
                if ref is ag0:
                    t0, t1 = ref[side, 2 * m, rem(xs - x + 4, 4)], ref[side, 2 * m + 1, rem(xs - x + 4, 4)]
                else:
                    t0, t1 = ref[side, xs, 2 * m], ref[side, xs, 2 * m + 1]
                low = lax.broadcasted_iota(jnp.int32, (size, 128), 1) < 64
                for top, value in (
                    (at, jnp.where(low, t0, pltpu.roll(t1, 64, 1))),
                    (HALF + at, jnp.where(low, pltpu.roll(t0, 64, 1), t1)),
                ):
                    high, rest = split(value)
                    ah[xs + 4 * side, top : top + size, lanes] = high
                    al[xs + 4 * side, top : top + size, lanes] = rest

    def prepare_range(lo, hi):
        def body(i, carry):
            prepare(i)
            return carry

        lax.fori_loop(lo, hi, body, 0)

    prepare_range(0, 8)
    both((), NE_LATER[0])
    prepare_range(8, 16)
    both((), NE_LATER[1])

    def product(t, s):
        near = jnp.where(t == 0, 0, jnp.where(t == 1, -2, jnp.where(t == 2, 2, 4)))
        odd = jnp.where(t == 0, -1, jnp.where(t == 1, 1, jnp.where(t == 2, -3, 3)))
        j = 2 * div(zz(jnp.where(eq, near, odd)), 2) + s
        keep = lax.broadcasted_iota(jnp.int32, (64, B), 0) < 60
        for k in range(8):
            value = jnp.where(keep, fg[j, 60 * k : 60 * k + 64, :], 0.0)
            high, rest = split(value)
            fph[64 * k : 64 * k + 64, :] = high
            fpl[64 * k : 64 * k + 64, :] = rest
        acc[...] += dot3((ah[j], al[j]), (fph[...], fpl[...]), ((1,), (0,)))

    def products(lo, hi):
        def body(i, carry):
            product(div(i, 2), rem(i, 2))
            return carry

        lax.fori_loop(lo, hi, body, 0)

    @pl.when(eq)
    def _():
        for q in range(NQ):
            f_wait(z, 1 - c, q)

    products(0, 2)
    both((), NE_LATER[2])
    products(2, 4)
    both((), NE_LATER[3])
    products(4, 6)
    for s in range(2):
        @pl.when(eq)
        def _():
            for q in range(NQ):
                f_wait(zz(4), s, q)

        products(6 + s, 7 + s)

    @pl.when(ne)
    def _():
        go(acc, cr, r_c.at[0], dev(x, y, 2 * zh + c, a), "ne")

    part[...] += dot3(split(fg[2 * zh + a, 0:SLAB, :]), split(acc[...]), ((0,), (0,)))

    @pl.when(ne)
    def _():
        go(part, pr, r_p.at[0], dev(x, y, zz(2 * a - 1), c), "ne")

    def give(k, core):
        owner = zz(2 * k)
        rows = pl.ds(pl.multiple_of(32 * (2 * div(owner, 2) + core), 32), 32)
        go(part.at[rows, :], dr.at[zh], r_d.at[zh], dev(x, y, owner, core), "eq")

    @pl.when(eq)
    def _():
        arrived(pr, r_p.at[0])
        part[...] += pr[...]
        for k in (2, 1, 3):
            give(k, c)
            give(k, 1 - c)
        give(0, 1 - c)

    @pl.when(eq)
    def _():
        dr[zh] = part[pl.ds(pl.multiple_of(32 * p, 32), 32), :]
        sel_v[...] = -masked(acc[...])

    @pl.when(ne)
    def _():
        arrived(cr, r_c.at[0])
        sel_v[...] = -masked(cr[...])

    sel_out = pltpu.make_async_copy(sel_v, sel_ref, local.at[0])
    sel_out.start()

    @pl.when(ne)
    def _():
        arrived(dr.at[zh], r_d.at[zh])

    for k in range(1, 4):
        arrived(dr.at[rem(zh + k, 4)], r_d.at[rem(zh + k, 4)])
    total = dr[0]
    for k in range(1, 4):
        total = total + dr[k]
    diag_v[...] = total
    diag_out = pltpu.make_async_copy(diag_v, diag_ref.at[0], local.at[1])
    diag_out.start()

    def finish(kind):
        like = {
            (CHUNK, B): fu.at[pl.ds(0, CHUNK), :],
            (U0, 128): ag0.at[0, 0, 0],
            (U1, 128): ag1.at[0, 0, 0],
            (1, U0, 128): ag0.at[0, 0, pl.ds(0, 1)],
            (3, U0, 128): ag0.at[0, 0, pl.ds(0, 3)],
            (B, B): part,
            (4, U0, 128): ag0.at[0, 0],
            (8, U1, 128): ag1.at[0, 0],
            (SLAB, B): acc,
            (32, B): lb.at[0],
        }
        for shape, index in pending[kind]:
            pltpu.make_async_remote_copy(
                src_ref=like[shape], dst_ref=like[shape], send_sem=send.at[index], recv_sem=r_l.at[0],
                device_id=sibling, device_id_type=MESH,
            ).wait_send()

    finish("all")

    @pl.when(eq)
    def _():
        finish("eq")

    @pl.when(ne)
    def _():
        finish("ne")

    sel_out.wait()
    diag_out.wait()


def hand_over(sel_ref, diag_ref, sel_out, diag_out):
    sel_out[...] = sel_ref[...]
    diag_out[...] = diag_ref[...]


def on_device(ancestor_inverse, factor, struct_rows, diag_factor_inverse):
    vmem = pl.BlockSpec(memory_space=pltpu.VMEM)
    anywhere = pl.BlockSpec(memory_space=pl.ANY)
    dma = pltpu.SemaphoreType.DMA
    shapes = (jax.ShapeDtypeStruct((SLAB, B), F32), jax.ShapeDtypeStruct((1, 32, B), F32))
    results = pl.pallas_call(
        kernel,
        out_shape=shapes,
        in_specs=[anywhere, anywhere, pl.BlockSpec(memory_space=pltpu.SMEM), anywhere],
        out_specs=(anywhere, anywhere),
        scratch_shapes=[
            pltpu.VMEM((SLAB, B), F32),
            pltpu.VMEM((32, B), F32),
            pltpu.VMEM((60, SLAB), F32),
            pltpu.VMEM((128, 512), F32),
            pltpu.VMEM((512, 128), F32),
            pltpu.VMEM((HALF, 128), F32),
            pltpu.VMEM((2, NY, NX, U0, 128), F32),
            pltpu.VMEM((2, NX, NY, U1, 128), F32),
            pltpu.VMEM((8, SLAB, 512), BF16),
            pltpu.VMEM((8, SLAB, 512), BF16),
            pltpu.VMEM((SLAB, B), F32),
            pltpu.VMEM((8, SLAB + 8, B), F32),
            pltpu.VMEM((512, B), BF16),
            pltpu.VMEM((512, B), BF16),
            pltpu.VMEM((SLAB, B), F32),
            pltpu.VMEM((SLAB, B), F32),
            pltpu.VMEM((2, 32, B), F32),
            pltpu.VMEM((B, B), F32),
            pltpu.VMEM((B, B), F32),
            pltpu.VMEM((4, 32, B), F32),
            dma((3,)),
            dma((256,)),
            dma((2,)),
            dma((3,)),
            dma((8,)),
            dma((14,)),
            dma((24,)),
            dma((8,)),
            dma((4,)),
            dma((8 * NQ,)),
            dma((1,)),
            dma((1,)),
            dma((1,)),
            dma((4,)),
        ],
        compiler_params=pltpu.CompilerParams(
            collective_id=0, has_side_effects=True, vmem_limit_bytes=60 * 1024 * 1024
        ),
    )(ancestor_inverse.T, factor, struct_rows, diag_factor_inverse)
    return pl.pallas_call(
        hand_over,
        out_shape=shapes,
        in_specs=[vmem, vmem],
        out_specs=(vmem, vmem),
    )(*results)


def solution(mesh):
    placed = (P("pcol", "prow"), P("pcol", "prow"), P("prow", None), P("prow", "pcol", None))
    return jax.shard_map(
        on_device,
        mesh=mesh,
        in_specs=placed,
        out_specs=(P("pcol", "prow"), P("prow", "pcol", None)),
        check_vma=False,
    )
```

```python
import jax
import jax.numpy as jnp
import numpy as np
from jax import lax
from jax.experimental import pallas as pl
from jax.experimental.pallas import tpu as pltpu
from jax.sharding import PartitionSpec as P

MESH = pl.DeviceIdType.MESH
F32 = jnp.float32
BF16 = jnp.bfloat16
NX, NY, NZ = 4, 8, 8
B = 256
SLAB = 480
HALF = 240
U0 = 64
U1 = 176
NQ = 4
CHUNK = SLAB // NQ
MOST = 4
EQ_FIRST = (
    ("own",), ("y1", 1), ("y1", -1), ("x0",), ("xp", -1), ("y1", -2), ("y1", 2), ("y0", 1, -1, 1), ("gram",),
    ("y0", 1, 1, 0), ("y0", 1, -1, 0), ("xp", 1), ("y1", -3), ("y1", 4), ("xp", -2), ("y0", 1, 1, 1), ("y0", 2, 1, 0),
    ("y1", 3), ("f2", 0, 1), ("f2", 0, -1), ("xp", 0), ("f2", 1, 1), ("y0", 2, -1, 1), ("y0", 3, 1, 0),
    ("y0", 2, -1, 0), ("f2", 1, -1), ("f2", 2, 1), ("y0", 2, 1, 1), ("xp", 2), ("sh", 0), ("xp", 3), ("f2", 2, -1),
    ("f2", 3, 1), ("y0", 3, -1, 0), ("xp", 4), ("xp", -3), ("f2", 3, -1), ("f2", 4, 1), ("y0", 4, 1, 0),
    ("f2", 4, -1), ("sh", 2), ("sh", 1), ("y0", 3, 1, 1), ("f2", 5, 1), ("f2", 5, -1), ("f2", 6, 1), ("sh", 3),
    ("f2", 6, -1), ("y0", 4, 1, 1), ("f2", 7, 1), ("f2", 7, -1), ("y0", 3, -1, 1),
)
NE_FIRST = (
    ("f1", 0, 1), ("a0",), ("y1", 1), ("f1", 0, -1), ("f1", 1, 1), ("f1", 1, -1), ("f1", 2, 1), ("x0",), ("y1", -1),
    ("f1", 2, -1), ("y1", 2), ("y0", 1, -1, 0), ("f1", 3, 1), ("y0", 1, 1, 0), ("f1", 3, -1), ("y1", -2),
    ("y0", 1, 1, 1), ("y1", 3), ("f1", 4, 1), ("f1", 4, -1), ("f1", 5, 1), ("y0", 2, -1, 0), ("xp", 0), ("f1", 5, -1),
    ("y1", -3), ("y0", 2, 1, 0), ("y1", 4), ("f1", 6, 1), ("f1", 6, -1), ("y0", 1, -1, 1), ("f1", 7, 1), ("xp", -2),
    ("sh", 0), ("xp", -1), ("xp", 2), ("xp", 1), ("y0", 2, 1, 1), ("f1", 7, -1), ("xp", -3), ("y0", 3, 1, 0),
    ("xp", 3), ("y0", 2, -1, 1), ("xp", 4), ("y0", 3, 1, 1), ("y0", 3, -1, 0), ("sh", 3), ("sh", 1), ("sh", 2),
    ("y0", 3, -1, 1), ("f3", 0), ("y0", 4, 1, 0), ("y0", 4, 1, 1),
)
NE_LATER = (
    (("f3", 1),),
    (("f3", 2),),
    (("f3", 3),),
    (("f3", 4), ("f3", 5), ("fr", 0), ("fr", 1), ("fr", 2), ("fr", 3)),
    (("f3", 6), ("f3", 7), ("fr", 4), ("fr", 5), ("fr", 6), ("fr", 7)),
)


def split(v):
    high = v.astype(BF16)
    return high, (v - high.astype(F32)).astype(BF16)


def dot3(left, right, dims):
    lh, ll = left
    rh, rl = right
    go = lambda p, q: lax.dot_general(p, q, (dims, ((), ())), preferred_element_type=F32)
    return go(lh, rh) + (go(ll, rh) + go(lh, rl))


def kernel(
    a_ref, f_ref, s_ref, d_ref, sel_ref, diag_ref,
    sel_v, diag_v, ta, tw, tz, pk, ag0, ag1, ah, al, fu, fg, fph, fpl, fth, ftl, acc, cr, lb, part, pr, dr,
    local, send, r_a0, r_x0, r_y1, r_y0, r_x1, r_s0, r_s1, r_f, r_l, r_c, r_p, r_d,
):
    def rem(value, by):
        return lax.rem(value, np.int32(by))

    def div(value, by):
        return lax.div(value, np.int32(by))

    r, p = lax.axis_index("prow"), lax.axis_index("pcol")
    a, x, y = div(r, 32), rem(div(r, 8), 4), rem(r, 8)
    zh, c = div(p, 2), rem(p, 2)
    z = 2 * zh + a
    eq, ne = a == c, a != c
    dsg = 1 - 2 * c
    xp, xm, x2 = rem(x + 4 + dsg, 4), rem(x + 4 - dsg, 4), rem(x + 2, 4)

    def yy(k):
        return rem(y + 16 + k * dsg, 8)

    def zz(k):
        return rem(z + 8 + k, 8)

    def dev(x_, y_, z_, c_):
        return (rem(z_, 2) * 32 + x_ * 8 + y_, div(z_, 2) * 2 + c_)

    counter = [0]
    pending = {"all": [], "eq": [], "ne": []}

    def go(src, dst, recv, device, kind="all"):
        copy = pltpu.make_async_remote_copy(
            src_ref=src, dst_ref=dst, send_sem=send.at[counter[0]], recv_sem=recv,
            device_id=device, device_id_type=MESH,
        )
        counter[0] += 1
        copy.start()
        pending[kind].append((src.shape, counter[0] - 1))

    sibling = dev(x, y, z, 1 - c)

    def arrived(dst, recv):
        pltpu.make_async_remote_copy(
            src_ref=dst, dst_ref=dst, send_sem=send.at[0], recv_sem=recv,
            device_id=sibling, device_id_type=MESH,
        ).wait_recv()

    loads = [
        pltpu.make_async_copy(a_ref, ta, local.at[0]),
        pltpu.make_async_copy(f_ref, fu, local.at[1]),
        pltpu.make_async_copy(d_ref.at[0], lb.at[0], local.at[2]),
    ]
    for load in loads:
        load.start()
    barrier = pltpu.get_barrier_semaphore()
    greeted = [sibling]
    for k in (1, -1):
        greeted += [dev(x, y, zz(k), 0), dev(x, y, zz(k), 1)]
    greeted += [dev(xp, y, z, c), dev(xm, y, z, c), dev(x2, y, z, c)]
    greeted += [dev(x, yy(k), z, c) for k in (1, -1, 2, -2)]
    for device in greeted:
        pl.semaphore_signal(barrier, inc=1, device_id=device, device_id_type=MESH)

    tw[...] = jnp.zeros_like(tw)
    for load in loads:
        load.wait()
    tw[0:60, 0:SLAB] = ta[...]
    tz[...] = jnp.transpose(tw[...])
    pk[...] = tz[0:HALF, :] + pltpu.roll(tz[HALF:SLAB, :], 64, 1)

    first = div(SLAB * p, B)

    def listed(block):
        total = np.float32(0.0)
        for i in range(s_ref.shape[1]):
            total = jnp.maximum(total, jnp.where(s_ref[0, i] == block, np.float32(1.0), np.float32(0.0)))
        return total

    present = [listed(first + i) for i in range(3)]

    def masked(value):
        block = (lax.broadcasted_iota(jnp.int32, (SLAB, B), 0) + SLAB * p) // B - first
        return value * jnp.where(block == 0, present[0], jnp.where(block == 1, present[1], present[2]))

    fu[...] = masked(fu[...])

    @pl.when(eq)
    def _():
        ag0[c, y, 0] = pk[0:U0, :]
        ag1[c, x, y] = pk[U0:HALF, :]

    row = lax.broadcasted_iota(jnp.int32, (32, B), 0) + 32 * p
    lb[0] = jnp.where(row >= lax.broadcasted_iota(jnp.int32, (32, B), 1), lb[0], 0.0)

    pl.semaphore_wait(barrier, len(greeted))

    @pl.when(ne)
    def _():
        partner = dev(x, y, 2 * zh + c, a)
        go(pk.at[pl.ds(0, U0), :], ag0.at[a, y, 0], r_a0.at[0], partner, "ne")
        go(pk.at[pl.ds(U0, U1), :], ag1.at[a, x, y], r_a0.at[1], partner, "ne")

    def fslot(j, q):
        return fg.at[j, pl.ds(CHUNK * q, CHUNK), :]

    for q in range(NQ):
        for sign in (1, -1):
            go(fu.at[pl.ds(CHUNK * q, CHUNK), :], fslot(p, q), r_f.at[NQ * p + q], dev(x, y, zz(sign), a))

    @pl.when(ne)
    def _():
        for q in range(NQ):
            go(fu.at[pl.ds(CHUNK * q, CHUNK), :], fslot(p, q), r_f.at[NQ * p + q], sibling, "ne")
        go(lb.at[0], lb.at[1], r_l.at[0], sibling, "ne")

    @pl.when(eq)
    def _():
        fg[p, 0:SLAB, :] = fu[...]

    acc[...] = jnp.zeros_like(acc)
    part[...] = jnp.zeros_like(part)

    def f_wait(source, s, q):
        j = 2 * div(source, 2) + s
        arrived(fslot(j, q), r_f.at[NQ * j + q])
        return j

    def f_pass(e, distance, sign, kind):
        s, q = e % 2, e // 2
        j = f_wait(zz(-distance * sign), s, q)
        go(fslot(j, q), fslot(j, q), r_f.at[NQ * j + q], dev(x, y, zz(sign), c), kind)

    def f1(e, sign):
        f_pass(e, 1, sign, "ne")

    def f2(e, sign):
        f_pass(e, 2, sign, "eq")

    def f3(e):
        s, q = e % 2, e // 2
        way = dsg if e < MOST else -dsg
        j = f_wait(zz(8 - 3 * way), s, q)
        go(fslot(j, q), fslot(j, q), r_f.at[NQ * j + q], dev(x, y, zz(way), c), "ne")

    def f3_rest(e):
        way = dsg if e < MOST else -dsg
        f_wait(zz(3 * way), e % 2, e // 2)

    to_xp, to_xm, to_x2 = dev(xp, y, z, c), dev(xm, y, z, c), dev(x2, y, z, c)

    def to_y(k):
        return dev(x, yy(k), z, c)

    def tile1(y_):
        return ag1.at[c, x, y_]

    def group0(y_, half):
        return ag0.at[c, y_, pl.ds(3 * half - 2 * half, 1 + 2 * half)]

    def along_x(k):
        src = tile1(yy(k))
        go(src, src, r_x1.at[yy(k)], to_xp, kind[0])
        go(src, src, r_x1.at[8 + yy(k)], to_xm, kind[0])

    def x1_pass(k):
        y_ = yy(k)
        if k in (0, -1, 2, -3):
            src = ag1.at[c, xm, y_]
            arrived(src, r_x1.at[y_])
            go(src, src, r_x1.at[16 + y_], to_xp, kind[0])
        else:
            src = ag1.at[c, xp, y_]
            arrived(src, r_x1.at[8 + y_])
            go(src, src, r_x1.at[16 + y_], to_xm, kind[0])

    def y1_wait(k):
        arrived(tile1(yy(-k)), r_y1.at[k + 3])

    def y1_go(own, k, kind):
        go(tile1(yy(own)), tile1(yy(own)), r_y1.at[k - own + 3], to_y(k), kind)

    def y0_go(k, sign, half):
        src = group0(yy(-sign * (k - 1)), half)
        go(src, src, r_y0.at[2 * (k - 1 + (0 if sign > 0 else 4)) + half], to_y(sign), kind[0])

    kind = ["all"]
    seen = set()

    def share0(y_):
        src = ag0.at[c, y_]
        go(src, src, r_s0.at[y_], sibling, kind[0])

    def share1(x_):
        src = ag1.at[c, x_]
        go(src, src, r_s1.at[x_], sibling, kind[0])

    def own_out():
        for k in (1, -1, 2, -2):
            y1_go(0, k, kind[0])
        src = ag0.at[c, y, 0]
        go(src, ag0.at[c, y, 2 + dsg], r_x0.at[0], to_xp, kind[0])
        go(src, ag0.at[c, y, 2 - dsg], r_x0.at[1], to_xm, kind[0])
        go(src, ag0.at[c, y, 2], r_x0.at[2], to_x2, kind[0])
        along_x(0)
        for sign in (1, -1):
            y0_go(1, sign, 0)

    def do_a0():
        arrived(ag0.at[c, y, 0], r_a0.at[0])
        arrived(ag1.at[c, x, y], r_a0.at[1])
        own_out()

    def do_x0():
        arrived(ag0.at[c, y, 2 + dsg], r_x0.at[0])
        arrived(ag0.at[c, y, 2 - dsg], r_x0.at[1])
        arrived(ag0.at[c, y, 2], r_x0.at[2])
        for sign in (1, -1):
            y0_go(1, sign, 1)
        share0(y)

    def do_y1(k):
        y1_wait(k)
        if k == 2:
            y1_go(-2, 1, kind[0])
            y1_go(-2, 2, kind[0])
        if k == -2:
            y1_go(2, -1, kind[0])
        along_x(4 if k == 4 else -k)

    def do_y0(k, sign, half):
        arrived(group0(yy(-sign * k), half), r_y0.at[2 * (k - 1 + (0 if sign > 0 else 4)) + half])
        if k < (4 if sign > 0 else 3):
            y0_go(k + 1, sign, half)
        if (k, sign) in seen:
            share0(yy(-sign * k))
        seen.add((k, sign))

    FROM_M = (0, -1, 2, -3)
    TILES = (0, 1, -1, 2, -2, 3, -3, 4)

    def do_share(which):
        if which == 0:
            share1(x)
        elif which == 1:
            for k in TILES:
                if k not in FROM_M:
                    arrived(ag1.at[c, xm, yy(k)], r_x1.at[yy(k)])
            share1(xm)
        elif which == 2:
            for k in TILES:
                if k in FROM_M:
                    arrived(ag1.at[c, xp, yy(k)], r_x1.at[8 + yy(k)])
            share1(xp)
        else:
            for k in TILES:
                arrived(ag1.at[c, x2, yy(k)], r_x1.at[16 + yy(k)])
            share1(x2)

    def gram():
        arrived(lb.at[1], r_l.at[0])
        total = jnp.zeros((B, B), F32)
        for i in range(2):
            piece = split(lb[i])
            total = total + dot3(piece, piece, ((0,), (0,)))
        part[...] = total

    steps = {
        "own": own_out, "a0": do_a0, "x0": do_x0, "y1": do_y1, "y0": do_y0, "xp": x1_pass, "sh": do_share,
        "f1": f1, "f2": f2, "f3": f3, "fr": f3_rest, "gram": gram,
    }

    def run(which, order):
        kind[0] = which
        seen.clear()
        for step in order:
            steps[step[0]](*step[1:])

    def both(order_eq, order_ne):
        @pl.when(eq)
        def _():
            run("eq", order_eq)

        @pl.when(ne)
        def _():
            run("ne", order_ne)

    both(EQ_FIRST, NE_FIRST)

    for k in range(8):
        arrived(ag0.at[1 - c, k], r_s0.at[k])
    for k in range(4):
        arrived(ag1.at[1 - c, k], r_s1.at[k])

    def prepare(i):
        xs = div(i, 4)
        m = rem(i, 4)
        lanes = pl.ds(pl.multiple_of(128 * m, 128), 128)
        for side in range(2):
            for ref, at, size in ((ag0, 0, U0), (ag1, U0, U1)):
                if ref is ag0:
                    t0, t1 = ref[side, 2 * m, rem(xs - x + 4, 4)], ref[side, 2 * m + 1, rem(xs - x + 4, 4)]
                else:
                    t0, t1 = ref[side, xs, 2 * m], ref[side, xs, 2 * m + 1]
                low = lax.broadcasted_iota(jnp.int32, (size, 128), 1) < 64
                for top, value in (
                    (at, jnp.where(low, t0, pltpu.roll(t1, 64, 1))),
                    (HALF + at, jnp.where(low, pltpu.roll(t0, 64, 1), t1)),
                ):
                    high, rest = split(value)
                    ah[xs + 4 * side, top : top + size, lanes] = high
                    al[xs + 4 * side, top : top + size, lanes] = rest

    def prepare_range(lo, hi):
        def body(i, carry):
            prepare(i)
            return carry

        lax.fori_loop(lo, hi, body, 0)

    prepare_range(0, 8)
    both((), NE_LATER[0])
    prepare_range(8, 16)
    both((), NE_LATER[1])

    fth[...], ftl[...] = split(jnp.transpose(fg[2 * zh + a]))

    def product(t, s, h):
        near = jnp.where(t == 0, 0, jnp.where(t == 1, -2, jnp.where(t == 2, 2, 4)))
        odd = jnp.where(t == 0, -1, jnp.where(t == 1, 1, jnp.where(t == 2, -3, 3)))
        j = 2 * div(zz(jnp.where(eq, near, odd)), 2) + s
        base = pl.multiple_of(HALF * h, 8)
        keep = lax.broadcasted_iota(jnp.int32, (64, B), 0) < 60
        for k in range(4):
            value = fg[j, pl.ds(pl.multiple_of(base + 60 * k - 4 * (k % 2), 8), 64), :]
            if k % 2:
                value = pltpu.roll(value, 60, 0)
            high, rest = split(jnp.where(keep, value, 0.0))
            fph[64 * k : 64 * k + 64, :] = high
            fpl[64 * k : 64 * k + 64, :] = rest
        lanes = pl.ds(pl.multiple_of(256 * h, 256), 256)
        acc[...] += dot3((ah[j, :, lanes], al[j, :, lanes]), (fph[...], fpl[...]), ((1,), (0,)))

    def products(count, pick):
        def body(i, carry):
            product(*pick(i))
            return carry

        lax.fori_loop(0, count, body, 0)

    @pl.when(eq)
    def _():
        for q in range(NQ):
            f_wait(z, 1 - c, q)

    def last_wait(h):
        @pl.when(eq)
        def _():
            for q in range(h * NQ // 2, (h + 1) * NQ // 2):
                for s in range(2):
                    f_wait(zz(4), s, q)

    products(4, lambda i: (0, div(i, 2), rem(i, 2)))
    both((), NE_LATER[2])
    products(4, lambda i: (1, div(i, 2), rem(i, 2)))
    both((), NE_LATER[3])
    products(2, lambda i: (2, i, 0))
    last_wait(0)
    products(2, lambda i: (3, i, 0))
    both((), NE_LATER[4])
    products(2, lambda i: (2, i, 1))
    last_wait(1)
    products(2, lambda i: (3, i, 1))

    @pl.when(ne)
    def _():
        go(acc, cr, r_c.at[0], dev(x, y, 2 * zh + c, a), "ne")

    part[...] += dot3((fth[...], ftl[...]), split(acc[...]), ((1,), (0,)))

    @pl.when(ne)
    def _():
        go(part, pr, r_p.at[0], dev(x, y, zz(2 * a - 1), c), "ne")

    def give(k, core):
        owner = zz(2 * k)
        rows = pl.ds(pl.multiple_of(32 * (2 * div(owner, 2) + core), 32), 32)
        go(part.at[rows, :], dr.at[zh], r_d.at[zh], dev(x, y, owner, core), "eq")

    @pl.when(eq)
    def _():
        arrived(pr, r_p.at[0])
        part[...] += pr[...]
        for k in (2, 1, 3):
            give(k, c)
            give(k, 1 - c)
        give(0, 1 - c)

    @pl.when(eq)
    def _():
        dr[zh] = part[pl.ds(pl.multiple_of(32 * p, 32), 32), :]
        sel_v[...] = -masked(acc[...])

    @pl.when(ne)
    def _():
        arrived(cr, r_c.at[0])
        sel_v[...] = -masked(cr[...])

    sel_out = pltpu.make_async_copy(sel_v, sel_ref, local.at[0])
    sel_out.start()

    @pl.when(ne)
    def _():
        arrived(dr.at[zh], r_d.at[zh])

    for k in range(1, 4):
        arrived(dr.at[rem(zh + k, 4)], r_d.at[rem(zh + k, 4)])
    total = dr[0]
    for k in range(1, 4):
        total = total + dr[k]
    diag_v[...] = total
    diag_out = pltpu.make_async_copy(diag_v, diag_ref.at[0], local.at[1])
    diag_out.start()

    def finish(kind):
        like = {
            (CHUNK, B): fu.at[pl.ds(0, CHUNK), :],
            (U0, 128): ag0.at[0, 0, 0],
            (U1, 128): ag1.at[0, 0, 0],
            (1, U0, 128): ag0.at[0, 0, pl.ds(0, 1)],
            (3, U0, 128): ag0.at[0, 0, pl.ds(0, 3)],
            (B, B): part,
            (4, U0, 128): ag0.at[0, 0],
            (8, U1, 128): ag1.at[0, 0],
            (SLAB, B): acc,
            (32, B): lb.at[0],
        }
        for shape, index in pending[kind]:
            pltpu.make_async_remote_copy(
                src_ref=like[shape], dst_ref=like[shape], send_sem=send.at[index], recv_sem=r_l.at[0],
                device_id=sibling, device_id_type=MESH,
            ).wait_send()

    finish("all")

    @pl.when(eq)
    def _():
        finish("eq")

    @pl.when(ne)
    def _():
        finish("ne")

    sel_out.wait()
    diag_out.wait()


def hand_over(sel_ref, diag_ref, sel_out, diag_out):
    sel_out[...] = sel_ref[...]
    diag_out[...] = diag_ref[...]


def on_device(ancestor_inverse, factor, struct_rows, diag_factor_inverse):
    vmem = pl.BlockSpec(memory_space=pltpu.VMEM)
    anywhere = pl.BlockSpec(memory_space=pl.ANY)
    dma = pltpu.SemaphoreType.DMA
    shapes = (jax.ShapeDtypeStruct((SLAB, B), F32), jax.ShapeDtypeStruct((1, 32, B), F32))
    results = pl.pallas_call(
        kernel,
        out_shape=shapes,
        in_specs=[anywhere, anywhere, pl.BlockSpec(memory_space=pltpu.SMEM), anywhere],
        out_specs=(anywhere, anywhere),
        scratch_shapes=[
            pltpu.VMEM((SLAB, B), F32),
            pltpu.VMEM((32, B), F32),
            pltpu.VMEM((60, SLAB), F32),
            pltpu.VMEM((128, 512), F32),
            pltpu.VMEM((512, 128), F32),
            pltpu.VMEM((HALF, 128), F32),
            pltpu.VMEM((2, NY, NX, U0, 128), F32),
            pltpu.VMEM((2, NX, NY, U1, 128), F32),
            pltpu.VMEM((8, SLAB, 512), BF16),
            pltpu.VMEM((8, SLAB, 512), BF16),
            pltpu.VMEM((SLAB, B), F32),
            pltpu.VMEM((8, SLAB, B), F32),
            pltpu.VMEM((256, B), BF16),
            pltpu.VMEM((256, B), BF16),
            pltpu.VMEM((B, SLAB), BF16),
            pltpu.VMEM((B, SLAB), BF16),
            pltpu.VMEM((SLAB, B), F32),
            pltpu.VMEM((SLAB, B), F32),
            pltpu.VMEM((2, 32, B), F32),
            pltpu.VMEM((B, B), F32),
            pltpu.VMEM((B, B), F32),
            pltpu.VMEM((4, 32, B), F32),
            dma((3,)),
            dma((256,)),
            dma((2,)),
            dma((3,)),
            dma((8,)),
            dma((14,)),
            dma((24,)),
            dma((8,)),
            dma((4,)),
            dma((8 * NQ,)),
            dma((1,)),
            dma((1,)),
            dma((1,)),
            dma((4,)),
        ],
        compiler_params=pltpu.CompilerParams(
            collective_id=0, has_side_effects=True, vmem_limit_bytes=60 * 1024 * 1024
        ),
    )(ancestor_inverse.T, factor, struct_rows, diag_factor_inverse)
    return pl.pallas_call(
        hand_over,
        out_shape=shapes,
        in_specs=[vmem, vmem],
        out_specs=(vmem, vmem),
    )(*results)


def solution(mesh):
    placed = (P("pcol", "prow"), P("pcol", "prow"), P("prow", None), P("prow", "pcol", None))
    return jax.shard_map(
        on_device,
        mesh=mesh,
        in_specs=placed,
        out_specs=(P("pcol", "prow"), P("prow", "pcol", None)),
        check_vma=False,
    )
```

```python
import jax
import jax.numpy as jnp
import numpy as np
from jax import lax
from jax.experimental import pallas as pl
from jax.experimental.pallas import tpu as pltpu
from jax.sharding import PartitionSpec as P

MESH = pl.DeviceIdType.MESH
F32 = jnp.float32
BF16 = jnp.bfloat16
NX, NY, NZ = 4, 8, 8
B = 256
SLAB = 480
HALF = 240
U0 = 64
U1 = 176
NQ = 4
CHUNK = SLAB // NQ
MOST = 4
EQ_FIRST = (
    ("own",), ("y1", 1), ("y1", -1), ("x0",), ("xp", -1), ("y1", -2), ("y1", 2), ("y0", 1, -1, 1), ("gram",),
    ("y0", 1, 1, 0), ("y0", 1, -1, 0), ("xp", 1), ("y1", -3), ("y1", 4), ("xp", -2), ("y0", 1, 1, 1), ("y0", 2, 1, 0),
    ("y1", 3), ("f2", 0, 1), ("f2", 0, -1), ("xp", 0), ("f2", 1, 1), ("y0", 2, -1, 1), ("y0", 3, 1, 0),
    ("y0", 2, -1, 0), ("f2", 1, -1), ("f2", 2, 1), ("y0", 2, 1, 1), ("xp", 2), ("sh", 0), ("xp", 3), ("f2", 2, -1),
    ("f2", 3, 1), ("y0", 3, -1, 0), ("xp", 4), ("xp", -3), ("f2", 3, -1), ("f2", 4, 1), ("y0", 4, 1, 0),
    ("f2", 4, -1), ("sh", 2), ("sh", 1), ("y0", 3, 1, 1), ("f2", 5, 1), ("f2", 5, -1), ("f2", 6, 1), ("sh", 3),
    ("f2", 6, -1), ("y0", 4, 1, 1), ("f2", 7, 1), ("f2", 7, -1), ("y0", 3, -1, 1),
)
NE_FIRST = (
    ("f1", 0, 1), ("a0",), ("y1", 1), ("f1", 0, -1), ("f1", 1, 1), ("f1", 1, -1), ("f1", 2, 1), ("x0",), ("y1", -1),
    ("f1", 2, -1), ("y1", 2), ("y0", 1, -1, 0), ("f1", 3, 1), ("y0", 1, 1, 0), ("f1", 3, -1), ("y1", -2),
    ("y0", 1, 1, 1), ("y1", 3), ("f1", 4, 1), ("f1", 4, -1), ("f1", 5, 1), ("y0", 2, -1, 0), ("xp", 0), ("f1", 5, -1),
    ("y1", -3), ("y0", 2, 1, 0), ("y1", 4), ("f1", 6, 1), ("f1", 6, -1), ("y0", 1, -1, 1), ("f1", 7, 1), ("xp", -2),
    ("sh", 0), ("xp", -1), ("xp", 2), ("xp", 1), ("y0", 2, 1, 1), ("f1", 7, -1), ("xp", -3), ("y0", 3, 1, 0),
    ("xp", 3), ("y0", 2, -1, 1), ("xp", 4), ("y0", 3, 1, 1), ("y0", 3, -1, 0), ("sh", 3), ("sh", 1), ("sh", 2),
    ("y0", 3, -1, 1), ("f3", 0), ("y0", 4, 1, 0), ("y0", 4, 1, 1),
)
NE_LATER = (
    (("f3", 1),),
    (("f3", 2),),
    (("f3", 3),),
    (("f3", 4), ("f3", 5), ("fr", 0), ("fr", 1), ("fr", 2), ("fr", 3)),
    (("f3", 6), ("f3", 7), ("fr", 4), ("fr", 5), ("fr", 6), ("fr", 7)),
)


def split(v):
    high = v.astype(BF16)
    return high, (v - high.astype(F32)).astype(BF16)


def dot3(left, right, dims):
    lh, ll = left
    rh, rl = right
    go = lambda p, q: lax.dot_general(p, q, (dims, ((), ())), preferred_element_type=F32)
    return go(lh, rh) + (go(ll, rh) + go(lh, rl))


def kernel(
    a_ref, f_ref, s_ref, d_ref, sel_ref, diag_ref,
    sel_v, diag_v, ta, tw, tz, pk, ag0, ag1, ah, al, fu, fg, fph, fpl, fwh, fwl, fth, ftl, acc, cr, lb, part, pr, dr,
    local, send, r_a0, r_x0, r_y1, r_y0, r_x1, r_s0, r_s1, r_f, r_l, r_c, r_p, r_d,
):
    def rem(value, by):
        return lax.rem(value, np.int32(by))

    def div(value, by):
        return lax.div(value, np.int32(by))

    r, p = lax.axis_index("prow"), lax.axis_index("pcol")
    a, x, y = div(r, 32), rem(div(r, 8), 4), rem(r, 8)
    zh, c = div(p, 2), rem(p, 2)
    z = 2 * zh + a
    eq, ne = a == c, a != c
    dsg = 1 - 2 * c
    xp, xm, x2 = rem(x + 4 + dsg, 4), rem(x + 4 - dsg, 4), rem(x + 2, 4)

    def yy(k):
        return rem(y + 16 + k * dsg, 8)

    def zz(k):
        return rem(z + 8 + k, 8)

    def dev(x_, y_, z_, c_):
        return (rem(z_, 2) * 32 + x_ * 8 + y_, div(z_, 2) * 2 + c_)

    counter = [0]
    pending = {"all": [], "eq": [], "ne": []}

    def go(src, dst, recv, device, kind="all"):
        copy = pltpu.make_async_remote_copy(
            src_ref=src, dst_ref=dst, send_sem=send.at[counter[0]], recv_sem=recv,
            device_id=device, device_id_type=MESH,
        )
        counter[0] += 1
        copy.start()
        pending[kind].append((src.shape, counter[0] - 1))

    sibling = dev(x, y, z, 1 - c)

    def arrived(dst, recv):
        pltpu.make_async_remote_copy(
            src_ref=dst, dst_ref=dst, send_sem=send.at[0], recv_sem=recv,
            device_id=sibling, device_id_type=MESH,
        ).wait_recv()

    loads = [
        pltpu.make_async_copy(a_ref, ta, local.at[0]),
        pltpu.make_async_copy(f_ref, fu, local.at[1]),
        pltpu.make_async_copy(d_ref.at[0], lb.at[0], local.at[2]),
    ]
    for load in loads:
        load.start()
    barrier = pltpu.get_barrier_semaphore()
    greeted = [sibling]
    for k in (1, -1):
        greeted += [dev(x, y, zz(k), 0), dev(x, y, zz(k), 1)]
    greeted += [dev(xp, y, z, c), dev(xm, y, z, c), dev(x2, y, z, c)]
    greeted += [dev(x, yy(k), z, c) for k in (1, -1, 2, -2)]
    for device in greeted:
        pl.semaphore_signal(barrier, inc=1, device_id=device, device_id_type=MESH)

    tw[...] = jnp.zeros_like(tw)
    for load in loads:
        load.wait()
    tw[0:60, 0:SLAB] = ta[...]
    tz[...] = jnp.transpose(tw[...])
    pk[...] = tz[0:HALF, :] + pltpu.roll(tz[HALF:SLAB, :], 64, 1)

    first = div(SLAB * p, B)

    def listed(block):
        total = np.float32(0.0)
        for i in range(s_ref.shape[1]):
            total = jnp.maximum(total, jnp.where(s_ref[0, i] == block, np.float32(1.0), np.float32(0.0)))
        return total

    present = [listed(first + i) for i in range(3)]

    def masked(value):
        block = (lax.broadcasted_iota(jnp.int32, (SLAB, B), 0) + SLAB * p) // B - first
        return value * jnp.where(block == 0, present[0], jnp.where(block == 1, present[1], present[2]))

    fu[...] = masked(fu[...])

    @pl.when(eq)
    def _():
        ag0[c, y, 0] = pk[0:U0, :]
        ag1[c, x, y] = pk[U0:HALF, :]

    row = lax.broadcasted_iota(jnp.int32, (32, B), 0) + 32 * p
    lb[0] = jnp.where(row >= lax.broadcasted_iota(jnp.int32, (32, B), 1), lb[0], 0.0)

    pl.semaphore_wait(barrier, len(greeted))

    @pl.when(ne)
    def _():
        partner = dev(x, y, 2 * zh + c, a)
        go(pk.at[pl.ds(0, U0), :], ag0.at[a, y, 0], r_a0.at[0], partner, "ne")
        go(pk.at[pl.ds(U0, U1), :], ag1.at[a, x, y], r_a0.at[1], partner, "ne")

    def fslot(j, q):
        return fg.at[j, pl.ds(CHUNK * q, CHUNK), :]

    for q in range(NQ):
        for sign in (1, -1):
            go(fu.at[pl.ds(CHUNK * q, CHUNK), :], fslot(p, q), r_f.at[NQ * p + q], dev(x, y, zz(sign), a))

    @pl.when(ne)
    def _():
        for q in range(NQ):
            go(fu.at[pl.ds(CHUNK * q, CHUNK), :], fslot(p, q), r_f.at[NQ * p + q], sibling, "ne")
        go(lb.at[0], lb.at[1], r_l.at[0], sibling, "ne")

    @pl.when(eq)
    def _():
        fg[p, 0:SLAB, :] = fu[...]

    acc[...] = jnp.zeros_like(acc)
    part[...] = jnp.zeros_like(part)

    def f_wait(source, s, q):
        j = 2 * div(source, 2) + s
        arrived(fslot(j, q), r_f.at[NQ * j + q])
        return j

    def f_pass(e, distance, sign, kind):
        s, q = e % 2, e // 2
        j = f_wait(zz(-distance * sign), s, q)
        go(fslot(j, q), fslot(j, q), r_f.at[NQ * j + q], dev(x, y, zz(sign), c), kind)

    def f1(e, sign):
        f_pass(e, 1, sign, "ne")

    def f2(e, sign):
        f_pass(e, 2, sign, "eq")

    def f3(e):
        s, q = e % 2, e // 2
        way = dsg if e < MOST else -dsg
        j = f_wait(zz(8 - 3 * way), s, q)
        go(fslot(j, q), fslot(j, q), r_f.at[NQ * j + q], dev(x, y, zz(way), c), "ne")

    def f3_rest(e):
        way = dsg if e < MOST else -dsg
        f_wait(zz(3 * way), e % 2, e // 2)

    to_xp, to_xm, to_x2 = dev(xp, y, z, c), dev(xm, y, z, c), dev(x2, y, z, c)

    def to_y(k):
        return dev(x, yy(k), z, c)

    def tile1(y_):
        return ag1.at[c, x, y_]

    def group0(y_, half):
        return ag0.at[c, y_, pl.ds(3 * half - 2 * half, 1 + 2 * half)]

    def along_x(k):
        src = tile1(yy(k))
        go(src, src, r_x1.at[yy(k)], to_xp, kind[0])
        go(src, src, r_x1.at[8 + yy(k)], to_xm, kind[0])

    def x1_pass(k):
        y_ = yy(k)
        if k in (0, -1, 2, -3):
            src = ag1.at[c, xm, y_]
            arrived(src, r_x1.at[y_])
            go(src, src, r_x1.at[16 + y_], to_xp, kind[0])
        else:
            src = ag1.at[c, xp, y_]
            arrived(src, r_x1.at[8 + y_])
            go(src, src, r_x1.at[16 + y_], to_xm, kind[0])

    def y1_wait(k):
        arrived(tile1(yy(-k)), r_y1.at[k + 3])

    def y1_go(own, k, kind):
        go(tile1(yy(own)), tile1(yy(own)), r_y1.at[k - own + 3], to_y(k), kind)

    def y0_go(k, sign, half):
        src = group0(yy(-sign * (k - 1)), half)
        go(src, src, r_y0.at[2 * (k - 1 + (0 if sign > 0 else 4)) + half], to_y(sign), kind[0])

    kind = ["all"]
    seen = set()

    def share0(y_):
        src = ag0.at[c, y_]
        go(src, src, r_s0.at[y_], sibling, kind[0])

    def share1(x_):
        src = ag1.at[c, x_]
        go(src, src, r_s1.at[x_], sibling, kind[0])

    def own_out():
        for k in (1, -1, 2, -2):
            y1_go(0, k, kind[0])
        src = ag0.at[c, y, 0]
        go(src, ag0.at[c, y, 2 + dsg], r_x0.at[0], to_xp, kind[0])
        go(src, ag0.at[c, y, 2 - dsg], r_x0.at[1], to_xm, kind[0])
        go(src, ag0.at[c, y, 2], r_x0.at[2], to_x2, kind[0])
        along_x(0)
        for sign in (1, -1):
            y0_go(1, sign, 0)

    def do_a0():
        arrived(ag0.at[c, y, 0], r_a0.at[0])
        arrived(ag1.at[c, x, y], r_a0.at[1])
        own_out()

    def do_x0():
        arrived(ag0.at[c, y, 2 + dsg], r_x0.at[0])
        arrived(ag0.at[c, y, 2 - dsg], r_x0.at[1])
        arrived(ag0.at[c, y, 2], r_x0.at[2])
        for sign in (1, -1):
            y0_go(1, sign, 1)
        share0(y)

    def do_y1(k):
        y1_wait(k)
        if k == 2:
            y1_go(-2, 1, kind[0])
            y1_go(-2, 2, kind[0])
        if k == -2:
            y1_go(2, -1, kind[0])
        along_x(4 if k == 4 else -k)

    def do_y0(k, sign, half):
        arrived(group0(yy(-sign * k), half), r_y0.at[2 * (k - 1 + (0 if sign > 0 else 4)) + half])
        if k < (4 if sign > 0 else 3):
            y0_go(k + 1, sign, half)
        if (k, sign) in seen:
            share0(yy(-sign * k))
        seen.add((k, sign))

    FROM_M = (0, -1, 2, -3)
    TILES = (0, 1, -1, 2, -2, 3, -3, 4)

    def do_share(which):
        if which == 0:
            share1(x)
        elif which == 1:
            for k in TILES:
                if k not in FROM_M:
                    arrived(ag1.at[c, xm, yy(k)], r_x1.at[yy(k)])
            share1(xm)
        elif which == 2:
            for k in TILES:
                if k in FROM_M:
                    arrived(ag1.at[c, xp, yy(k)], r_x1.at[8 + yy(k)])
            share1(xp)
        else:
            for k in TILES:
                arrived(ag1.at[c, x2, yy(k)], r_x1.at[16 + yy(k)])
            share1(x2)

    def gram():
        arrived(lb.at[1], r_l.at[0])
        total = jnp.zeros((B, B), F32)
        for i in range(2):
            piece = split(lb[i])
            total = total + dot3(piece, piece, ((0,), (0,)))
        part[...] = total

    steps = {
        "own": own_out, "a0": do_a0, "x0": do_x0, "y1": do_y1, "y0": do_y0, "xp": x1_pass, "sh": do_share,
        "f1": f1, "f2": f2, "f3": f3, "fr": f3_rest, "gram": gram,
    }

    def run(which, order):
        kind[0] = which
        seen.clear()
        for step in order:
            steps[step[0]](*step[1:])

    def both(order_eq, order_ne):
        @pl.when(eq)
        def _():
            run("eq", order_eq)

        @pl.when(ne)
        def _():
            run("ne", order_ne)

    both(EQ_FIRST, NE_FIRST)

    for k in range(8):
        arrived(ag0.at[1 - c, k], r_s0.at[k])
    for k in range(4):
        arrived(ag1.at[1 - c, k], r_s1.at[k])

    def prepare(i):
        xs = div(i, 4)
        m = rem(i, 4)
        lanes = pl.ds(pl.multiple_of(128 * m, 128), 128)
        for side in range(2):
            for ref, at, size in ((ag0, 0, U0), (ag1, U0, U1)):
                if ref is ag0:
                    t0, t1 = ref[side, 2 * m, rem(xs - x + 4, 4)], ref[side, 2 * m + 1, rem(xs - x + 4, 4)]
                else:
                    t0, t1 = ref[side, xs, 2 * m], ref[side, xs, 2 * m + 1]
                low = lax.broadcasted_iota(jnp.int32, (size, 128), 1) < 64
                for top, value in (
                    (at, jnp.where(low, t0, pltpu.roll(t1, 64, 1))),
                    (HALF + at, jnp.where(low, pltpu.roll(t0, 64, 1), t1)),
                ):
                    high, rest = split(value)
                    ah[xs + 4 * side, top : top + size, lanes] = high
                    al[xs + 4 * side, top : top + size, lanes] = rest

    def prepare_range(lo, hi):
        def body(i, carry):
            prepare(i)
            return carry

        lax.fori_loop(lo, hi, body, 0)

    prepare_range(0, 8)
    both((), NE_LATER[0])
    prepare_range(8, 16)
    both((), NE_LATER[1])

    fth[...], ftl[...] = split(jnp.transpose(fg[2 * zh + a]))

    def product(t, s, h):
        near = jnp.where(t == 0, 0, jnp.where(t == 1, -2, jnp.where(t == 2, 2, 4)))
        odd = jnp.where(t == 0, -1, jnp.where(t == 1, 1, jnp.where(t == 2, -3, 3)))
        j = 2 * div(zz(jnp.where(eq, near, odd)), 2) + s
        base = pl.multiple_of(HALF * h, 8)
        keep = lax.broadcasted_iota(jnp.int32, (64, B), 0) < 60
        for k in range(4):
            value = fg[j, pl.ds(pl.multiple_of(base + 60 * k - 4 * (k % 2), 8), 64), :]
            if k % 2:
                value = pltpu.roll(value, 60, 0)
            high, rest = split(jnp.where(keep, value, 0.0))
            fph[64 * k : 64 * k + 64, :] = high
            fpl[64 * k : 64 * k + 64, :] = rest
        lanes = pl.ds(pl.multiple_of(256 * h, 256), 256)
        acc[...] += dot3((ah[j, :, lanes], al[j, :, lanes]), (fph[...], fpl[...]), ((1,), (0,)))

    def whole(t):
        def body(s, carry):
            near = jnp.where(t == 0, 0, -2)
            odd = jnp.where(t == 0, -1, 1)
            j = 2 * div(zz(jnp.where(eq, near, odd)), 2) + s
            keep = lax.broadcasted_iota(jnp.int32, (64, B), 0) < 60
            for k in range(8):
                start = 60 * k - 4 * (k % 2)
                value = fg[j, start : start + 64, :]
                if k % 2:
                    value = pltpu.roll(value, 60, 0)
                high, rest = split(jnp.where(keep, value, 0.0))
                fwh[64 * k : 64 * k + 64, :] = high
                fwl[64 * k : 64 * k + 64, :] = rest
            acc[...] += dot3((ah[j], al[j]), (fwh[...], fwl[...]), ((1,), (0,)))
            return carry

        lax.fori_loop(0, 2, body, 0)

    def products(count, pick):
        def body(i, carry):
            product(*pick(i))
            return carry

        lax.fori_loop(0, count, body, 0)

    @pl.when(eq)
    def _():
        for q in range(NQ):
            f_wait(z, 1 - c, q)

    def last_wait(h):
        @pl.when(eq)
        def _():
            for q in range(h * NQ // 2, (h + 1) * NQ // 2):
                for s in range(2):
                    f_wait(zz(4), s, q)

    whole(0)
    both((), NE_LATER[2])
    whole(1)
    both((), NE_LATER[3])
    products(2, lambda i: (2, i, 0))
    last_wait(0)
    products(2, lambda i: (3, i, 0))
    both((), NE_LATER[4])
    products(2, lambda i: (2, i, 1))
    last_wait(1)
    products(2, lambda i: (3, i, 1))

    @pl.when(ne)
    def _():
        go(acc, cr, r_c.at[0], dev(x, y, 2 * zh + c, a), "ne")

    part[...] += dot3((fth[...], ftl[...]), split(acc[...]), ((1,), (0,)))

    @pl.when(ne)
    def _():
        go(part, pr, r_p.at[0], dev(x, y, zz(2 * a - 1), c), "ne")

    def give(k, core):
        owner = zz(2 * k)
        rows = pl.ds(pl.multiple_of(32 * (2 * div(owner, 2) + core), 32), 32)
        go(part.at[rows, :], dr.at[zh], r_d.at[zh], dev(x, y, owner, core), "eq")

    @pl.when(eq)
    def _():
        arrived(pr, r_p.at[0])
        part[...] += pr[...]
        for k in (2, 1, 3):
            give(k, c)
            give(k, 1 - c)
        give(0, 1 - c)

    @pl.when(eq)
    def _():
        dr[zh] = part[pl.ds(pl.multiple_of(32 * p, 32), 32), :]
        sel_v[...] = -masked(acc[...])

    @pl.when(ne)
    def _():
        arrived(cr, r_c.at[0])
        sel_v[...] = -masked(cr[...])

    sel_out = pltpu.make_async_copy(sel_v, sel_ref, local.at[0])
    sel_out.start()

    @pl.when(ne)
    def _():
        arrived(dr.at[zh], r_d.at[zh])

    for k in range(1, 4):
        arrived(dr.at[rem(zh + k, 4)], r_d.at[rem(zh + k, 4)])
    total = dr[0]
    for k in range(1, 4):
        total = total + dr[k]
    diag_v[...] = total
    diag_out = pltpu.make_async_copy(diag_v, diag_ref.at[0], local.at[1])
    diag_out.start()

    def finish(kind):
        like = {
            (CHUNK, B): fu.at[pl.ds(0, CHUNK), :],
            (U0, 128): ag0.at[0, 0, 0],
            (U1, 128): ag1.at[0, 0, 0],
            (1, U0, 128): ag0.at[0, 0, pl.ds(0, 1)],
            (3, U0, 128): ag0.at[0, 0, pl.ds(0, 3)],
            (B, B): part,
            (4, U0, 128): ag0.at[0, 0],
            (8, U1, 128): ag1.at[0, 0],
            (SLAB, B): acc,
            (32, B): lb.at[0],
        }
        for shape, index in pending[kind]:
            pltpu.make_async_remote_copy(
                src_ref=like[shape], dst_ref=like[shape], send_sem=send.at[index], recv_sem=r_l.at[0],
                device_id=sibling, device_id_type=MESH,
            ).wait_send()

    finish("all")

    @pl.when(eq)
    def _():
        finish("eq")

    @pl.when(ne)
    def _():
        finish("ne")

    sel_out.wait()
    diag_out.wait()


def hand_over(sel_ref, diag_ref, sel_out, diag_out):
    sel_out[...] = sel_ref[...]
    diag_out[...] = diag_ref[...]


def on_device(ancestor_inverse, factor, struct_rows, diag_factor_inverse):
    vmem = pl.BlockSpec(memory_space=pltpu.VMEM)
    anywhere = pl.BlockSpec(memory_space=pl.ANY)
    dma = pltpu.SemaphoreType.DMA
    shapes = (jax.ShapeDtypeStruct((SLAB, B), F32), jax.ShapeDtypeStruct((1, 32, B), F32))
    results = pl.pallas_call(
        kernel,
        out_shape=shapes,
        in_specs=[anywhere, anywhere, pl.BlockSpec(memory_space=pltpu.SMEM), anywhere],
        out_specs=(anywhere, anywhere),
        scratch_shapes=[
            pltpu.VMEM((SLAB, B), F32),
            pltpu.VMEM((32, B), F32),
            pltpu.VMEM((60, SLAB), F32),
            pltpu.VMEM((128, 512), F32),
            pltpu.VMEM((512, 128), F32),
            pltpu.VMEM((HALF, 128), F32),
            pltpu.VMEM((2, NY, NX, U0, 128), F32),
            pltpu.VMEM((2, NX, NY, U1, 128), F32),
            pltpu.VMEM((8, SLAB, 512), BF16),
            pltpu.VMEM((8, SLAB, 512), BF16),
            pltpu.VMEM((SLAB, B), F32),
            pltpu.VMEM((8, SLAB, B), F32),
            pltpu.VMEM((256, B), BF16),
            pltpu.VMEM((256, B), BF16),
            pltpu.VMEM((512, B), BF16),
            pltpu.VMEM((512, B), BF16),
            pltpu.VMEM((B, SLAB), BF16),
            pltpu.VMEM((B, SLAB), BF16),
            pltpu.VMEM((SLAB, B), F32),
            pltpu.VMEM((SLAB, B), F32),
            pltpu.VMEM((2, 32, B), F32),
            pltpu.VMEM((B, B), F32),
            pltpu.VMEM((B, B), F32),
            pltpu.VMEM((4, 32, B), F32),
            dma((3,)),
            dma((256,)),
            dma((2,)),
            dma((3,)),
            dma((8,)),
            dma((14,)),
            dma((24,)),
            dma((8,)),
            dma((4,)),
            dma((8 * NQ,)),
            dma((1,)),
            dma((1,)),
            dma((1,)),
            dma((4,)),
        ],
        compiler_params=pltpu.CompilerParams(
            collective_id=0, has_side_effects=True, vmem_limit_bytes=60 * 1024 * 1024
        ),
    )(ancestor_inverse.T, factor, struct_rows, diag_factor_inverse)
    return pl.pallas_call(
        hand_over,
        out_shape=shapes,
        in_specs=[vmem, vmem],
        out_specs=(vmem, vmem),
    )(*results)


def solution(mesh):
    placed = (P("pcol", "prow"), P("pcol", "prow"), P("prow", None), P("prow", "pcol", None))
    return jax.shard_map(
        on_device,
        mesh=mesh,
        in_specs=placed,
        out_specs=(P("pcol", "prow"), P("prow", "pcol", None)),
        check_vma=False,
    )
```

```python
import jax
import jax.numpy as jnp
import numpy as np
from jax import lax
from jax.experimental import pallas as pl
from jax.experimental.pallas import tpu as pltpu
from jax.sharding import PartitionSpec as P

MESH = pl.DeviceIdType.MESH
F32 = jnp.float32
BF16 = jnp.bfloat16
NX, NY, NZ = 4, 8, 8
B = 256
SLAB = 480
HALF = 240
U0 = 64
U1 = 176
NQ = 4
CHUNK = SLAB // NQ
MOST = 4
EQ_FIRST = (
    ("own",), ("y1", 1), ("y1", -1), ("x0",), ("xp", -1), ("y1", -2), ("y1", 2), ("y0", 1, -1, 1), ("gram",),
    ("y0", 1, 1, 0), ("y0", 1, -1, 0), ("xp", 1), ("y1", -3), ("y1", 4), ("xp", -2), ("y0", 1, 1, 1), ("y0", 2, 1, 0),
    ("y1", 3), ("f2", 0, 1), ("f2", 0, -1), ("xp", 0), ("f2", 1, 1), ("y0", 2, -1, 1), ("y0", 3, 1, 0),
    ("y0", 2, -1, 0), ("f2", 1, -1), ("f2", 2, 1), ("y0", 2, 1, 1), ("xp", 2), ("sh", 0), ("xp", 3), ("f2", 2, -1),
    ("f2", 3, 1), ("y0", 3, -1, 0), ("xp", 4), ("xp", -3), ("f2", 3, -1), ("f2", 4, 1), ("y0", 4, 1, 0),
    ("f2", 4, -1), ("sh", 2), ("sh", 1), ("y0", 3, 1, 1), ("f2", 5, 1), ("f2", 5, -1), ("f2", 6, 1), ("sh", 3),
    ("f2", 6, -1), ("y0", 4, 1, 1), ("f2", 7, 1), ("f2", 7, -1), ("y0", 3, -1, 1),
)
NE_FIRST = (
    ("f1", 0, 1), ("a0",), ("y1", 1), ("f1", 0, -1), ("f1", 1, 1), ("f1", 1, -1), ("f1", 2, 1), ("x0",), ("y1", -1),
    ("f1", 2, -1), ("y1", 2), ("y0", 1, -1, 0), ("f1", 3, 1), ("y0", 1, 1, 0), ("f1", 3, -1), ("y1", -2),
    ("y0", 1, 1, 1), ("y1", 3), ("f1", 4, 1), ("f1", 4, -1), ("f1", 5, 1), ("y0", 2, -1, 0), ("xp", 0), ("f1", 5, -1),
    ("y1", -3), ("y0", 2, 1, 0), ("y1", 4), ("f1", 6, 1), ("f1", 6, -1), ("y0", 1, -1, 1), ("f1", 7, 1), ("xp", -2),
    ("sh", 0), ("xp", -1), ("xp", 2), ("xp", 1), ("y0", 2, 1, 1), ("f1", 7, -1), ("xp", -3), ("y0", 3, 1, 0),
    ("xp", 3), ("y0", 2, -1, 1), ("xp", 4), ("y0", 3, 1, 1), ("y0", 3, -1, 0), ("sh", 3), ("sh", 1), ("sh", 2),
    ("y0", 3, -1, 1), ("f3", 0), ("y0", 4, 1, 0), ("y0", 4, 1, 1),
)
NE_LATER = (
    (("f3", 1),),
    (("f3", 2),),
    (("f3", 3),),
    (("f3", 4), ("f3", 5), ("fr", 0), ("fr", 1), ("fr", 2), ("fr", 3)),
    (("f3", 6), ("f3", 7), ("fr", 4), ("fr", 5), ("fr", 6), ("fr", 7)),
)


def split(v):
    high = v.astype(BF16)
    return high, (v - high.astype(F32)).astype(BF16)


def dot3(left, right, dims):
    lh, ll = left
    rh, rl = right
    go = lambda p, q: lax.dot_general(p, q, (dims, ((), ())), preferred_element_type=F32)
    return go(lh, rh) + (go(ll, rh) + go(lh, rl))


def kernel(
    a_ref, f_ref, s_ref, d_ref, sel_ref, diag_ref,
    sel_v, diag_v, ta, tw, tz, pk, ag0, ag1, ah, al, fu, fg, fph, fpl, fwh, fwl, fth, ftl, acc, cr, lb, part, pr, dr,
    local, send, r_a0, r_x0, r_y1, r_y0, r_x1, r_s0, r_s1, r_f, r_l, r_c, r_p, r_d,
):
    def rem(value, by):
        return lax.rem(value, np.int32(by))

    def div(value, by):
        return lax.div(value, np.int32(by))

    r, p = lax.axis_index("prow"), lax.axis_index("pcol")
    a, x, y = div(r, 32), rem(div(r, 8), 4), rem(r, 8)
    zh, c = div(p, 2), rem(p, 2)
    z = 2 * zh + a
    eq, ne = a == c, a != c
    dsg = 1 - 2 * c
    xp, xm, x2 = rem(x + 4 + dsg, 4), rem(x + 4 - dsg, 4), rem(x + 2, 4)

    def yy(k):
        return rem(y + 16 + k * dsg, 8)

    def zz(k):
        return rem(z + 8 + k, 8)

    def dev(x_, y_, z_, c_):
        return (rem(z_, 2) * 32 + x_ * 8 + y_, div(z_, 2) * 2 + c_)

    counter = [0]
    pending = {"all": [], "eq": [], "ne": []}

    def go(src, dst, recv, device, kind="all"):
        copy = pltpu.make_async_remote_copy(
            src_ref=src, dst_ref=dst, send_sem=send.at[counter[0]], recv_sem=recv,
            device_id=device, device_id_type=MESH,
        )
        counter[0] += 1
        copy.start()
        pending[kind].append((src.shape, counter[0] - 1))

    sibling = dev(x, y, z, 1 - c)

    def arrived(dst, recv):
        pltpu.make_async_remote_copy(
            src_ref=dst, dst_ref=dst, send_sem=send.at[0], recv_sem=recv,
            device_id=sibling, device_id_type=MESH,
        ).wait_recv()

    loads = [
        pltpu.make_async_copy(a_ref, ta, local.at[0]),
        pltpu.make_async_copy(f_ref, fu, local.at[1]),
        pltpu.make_async_copy(d_ref.at[0], lb.at[0], local.at[2]),
    ]
    for load in loads:
        load.start()
    barrier = pltpu.get_barrier_semaphore()
    greeted = [sibling]
    for k in (1, -1):
        greeted += [dev(x, y, zz(k), 0), dev(x, y, zz(k), 1)]
    greeted += [dev(xp, y, z, c), dev(xm, y, z, c), dev(x2, y, z, c)]
    greeted += [dev(x, yy(k), z, c) for k in (1, -1, 2, -2)]
    for device in greeted:
        pl.semaphore_signal(barrier, inc=1, device_id=device, device_id_type=MESH)

    tw[...] = jnp.zeros_like(tw)
    for load in loads:
        load.wait()
    tw[0:60, 0:SLAB] = ta[...]
    tz[...] = jnp.transpose(tw[...])
    pk[...] = tz[0:HALF, :] + pltpu.roll(tz[HALF:SLAB, :], 64, 1)

    first = div(SLAB * p, B)

    def listed(block):
        total = np.float32(0.0)
        for i in range(s_ref.shape[1]):
            total = jnp.maximum(total, jnp.where(s_ref[0, i] == block, np.float32(1.0), np.float32(0.0)))
        return total

    present = [listed(first + i) for i in range(3)]

    def masked(value):
        block = (lax.broadcasted_iota(jnp.int32, (SLAB, B), 0) + SLAB * p) // B - first
        return value * jnp.where(block == 0, present[0], jnp.where(block == 1, present[1], present[2]))

    fu[...] = masked(fu[...])

    @pl.when(eq)
    def _():
        ag0[c, y, 0] = pk[0:U0, :]
        ag1[c, x, y] = pk[U0:HALF, :]

    row = lax.broadcasted_iota(jnp.int32, (32, B), 0) + 32 * p
    lb[0] = jnp.where(row >= lax.broadcasted_iota(jnp.int32, (32, B), 1), lb[0], 0.0)

    pl.semaphore_wait(barrier, len(greeted))

    @pl.when(ne)
    def _():
        partner = dev(x, y, 2 * zh + c, a)
        go(pk.at[pl.ds(0, U0), :], ag0.at[a, y, 0], r_a0.at[0], partner, "ne")
        go(pk.at[pl.ds(U0, U1), :], ag1.at[a, x, y], r_a0.at[1], partner, "ne")

    def fslot(j, q):
        return fg.at[j, pl.ds(CHUNK * q, CHUNK), :]

    for q in range(NQ):
        for sign in (1, -1):
            go(fu.at[pl.ds(CHUNK * q, CHUNK), :], fslot(p, q), r_f.at[NQ * p + q], dev(x, y, zz(sign), a))

    @pl.when(ne)
    def _():
        for q in range(NQ):
            go(fu.at[pl.ds(CHUNK * q, CHUNK), :], fslot(p, q), r_f.at[NQ * p + q], sibling, "ne")
        go(lb.at[0], lb.at[1], r_l.at[0], sibling, "ne")

    @pl.when(eq)
    def _():
        fg[p, 0:SLAB, :] = fu[...]

    acc[...] = jnp.zeros_like(acc)
    part[...] = jnp.zeros_like(part)

    def f_wait(source, s, q):
        j = 2 * div(source, 2) + s
        arrived(fslot(j, q), r_f.at[NQ * j + q])
        return j

    def f_pass(e, distance, sign, kind):
        s, q = e % 2, e // 2
        j = f_wait(zz(-distance * sign), s, q)
        go(fslot(j, q), fslot(j, q), r_f.at[NQ * j + q], dev(x, y, zz(sign), c), kind)

    def f1(e, sign):
        f_pass(e, 1, sign, "ne")

    def f2(e, sign):
        f_pass(e, 2, sign, "eq")

    def f3(e):
        s, q = e % 2, e // 2
        way = dsg if e < MOST else -dsg
        j = f_wait(zz(8 - 3 * way), s, q)
        go(fslot(j, q), fslot(j, q), r_f.at[NQ * j + q], dev(x, y, zz(way), c), "ne")

    def f3_rest(e):
        way = dsg if e < MOST else -dsg
        f_wait(zz(3 * way), e % 2, e // 2)

    to_xp, to_xm, to_x2 = dev(xp, y, z, c), dev(xm, y, z, c), dev(x2, y, z, c)

    def to_y(k):
        return dev(x, yy(k), z, c)

    def tile1(y_):
        return ag1.at[c, x, y_]

    def group0(y_, half):
        return ag0.at[c, y_, pl.ds(3 * half - 2 * half, 1 + 2 * half)]

    def along_x(k):
        src = tile1(yy(k))
        go(src, src, r_x1.at[yy(k)], to_xp, kind[0])
        go(src, src, r_x1.at[8 + yy(k)], to_xm, kind[0])

    def x1_pass(k):
        y_ = yy(k)
        if k in (0, -1, 2, -3):
            src = ag1.at[c, xm, y_]
            arrived(src, r_x1.at[y_])
            go(src, src, r_x1.at[16 + y_], to_xp, kind[0])
        else:
            src = ag1.at[c, xp, y_]
            arrived(src, r_x1.at[8 + y_])
            go(src, src, r_x1.at[16 + y_], to_xm, kind[0])

    def y1_wait(k):
        arrived(tile1(yy(-k)), r_y1.at[k + 3])

    def y1_go(own, k, kind):
        go(tile1(yy(own)), tile1(yy(own)), r_y1.at[k - own + 3], to_y(k), kind)

    def y0_go(k, sign, half):
        src = group0(yy(-sign * (k - 1)), half)
        go(src, src, r_y0.at[2 * (k - 1 + (0 if sign > 0 else 4)) + half], to_y(sign), kind[0])

    kind = ["all"]
    seen = set()

    def share0(y_):
        src = ag0.at[c, y_]
        go(src, src, r_s0.at[y_], sibling, kind[0])

    def share1(x_):
        src = ag1.at[c, x_]
        go(src, src, r_s1.at[x_], sibling, kind[0])

    def own_out():
        for k in (1, -1, 2, -2):
            y1_go(0, k, kind[0])
        src = ag0.at[c, y, 0]
        go(src, ag0.at[c, y, 2 + dsg], r_x0.at[0], to_xp, kind[0])
        go(src, ag0.at[c, y, 2 - dsg], r_x0.at[1], to_xm, kind[0])
        go(src, ag0.at[c, y, 2], r_x0.at[2], to_x2, kind[0])
        along_x(0)
        for sign in (1, -1):
            y0_go(1, sign, 0)

    def do_a0():
        arrived(ag0.at[c, y, 0], r_a0.at[0])
        arrived(ag1.at[c, x, y], r_a0.at[1])
        own_out()

    def do_x0():
        arrived(ag0.at[c, y, 2 + dsg], r_x0.at[0])
        arrived(ag0.at[c, y, 2 - dsg], r_x0.at[1])
        arrived(ag0.at[c, y, 2], r_x0.at[2])
        for sign in (1, -1):
            y0_go(1, sign, 1)
        share0(y)

    def do_y1(k):
        y1_wait(k)
        if k == 2:
            y1_go(-2, 1, kind[0])
            y1_go(-2, 2, kind[0])
        if k == -2:
            y1_go(2, -1, kind[0])
        along_x(4 if k == 4 else -k)

    def do_y0(k, sign, half):
        arrived(group0(yy(-sign * k), half), r_y0.at[2 * (k - 1 + (0 if sign > 0 else 4)) + half])
        if k < (4 if sign > 0 else 3):
            y0_go(k + 1, sign, half)
        if (k, sign) in seen:
            share0(yy(-sign * k))
        seen.add((k, sign))

    FROM_M = (0, -1, 2, -3)
    TILES = (0, 1, -1, 2, -2, 3, -3, 4)

    def do_share(which):
        if which == 0:
            share1(x)
        elif which == 1:
            for k in TILES:
                if k not in FROM_M:
                    arrived(ag1.at[c, xm, yy(k)], r_x1.at[yy(k)])
            share1(xm)
        elif which == 2:
            for k in TILES:
                if k in FROM_M:
                    arrived(ag1.at[c, xp, yy(k)], r_x1.at[8 + yy(k)])
            share1(xp)
        else:
            for k in TILES:
                arrived(ag1.at[c, x2, yy(k)], r_x1.at[16 + yy(k)])
            share1(x2)

    def gram():
        arrived(lb.at[1], r_l.at[0])
        total = jnp.zeros((B, B), F32)
        for i in range(2):
            piece = split(lb[i])
            total = total + dot3(piece, piece, ((0,), (0,)))
        part[...] = total

    steps = {
        "own": own_out, "a0": do_a0, "x0": do_x0, "y1": do_y1, "y0": do_y0, "xp": x1_pass, "sh": do_share,
        "f1": f1, "f2": f2, "f3": f3, "fr": f3_rest, "gram": gram,
    }

    def run(which, order):
        kind[0] = which
        seen.clear()
        for step in order:
            steps[step[0]](*step[1:])

    def both(order_eq, order_ne):
        @pl.when(eq)
        def _():
            run("eq", order_eq)

        @pl.when(ne)
        def _():
            run("ne", order_ne)

    both(EQ_FIRST, NE_FIRST)

    for k in range(8):
        arrived(ag0.at[1 - c, k], r_s0.at[k])
    for k in range(4):
        arrived(ag1.at[1 - c, k], r_s1.at[k])

    def prepare(i):
        xs = div(i, 4)
        m = rem(i, 4)
        lanes = pl.ds(pl.multiple_of(128 * m, 128), 128)
        for side in range(2):
            for ref, at, size in ((ag0, 0, U0), (ag1, U0, U1)):
                if ref is ag0:
                    t0, t1 = ref[side, 2 * m, rem(xs - x + 4, 4)], ref[side, 2 * m + 1, rem(xs - x + 4, 4)]
                else:
                    t0, t1 = ref[side, xs, 2 * m], ref[side, xs, 2 * m + 1]
                low = lax.broadcasted_iota(jnp.int32, (size, 128), 1) < 64
                for top, value in (
                    (at, jnp.where(low, t0, pltpu.roll(t1, 64, 1))),
                    (HALF + at, jnp.where(low, pltpu.roll(t0, 64, 1), t1)),
                ):
                    high, rest = split(value)
                    ah[xs + 4 * side, top : top + size, lanes] = high
                    al[xs + 4 * side, top : top + size, lanes] = rest

    def prepare_range(lo, hi):
        def body(i, carry):
            prepare(i)
            return carry

        lax.fori_loop(lo, hi, body, 0)

    prepare_range(0, 8)
    both((), NE_LATER[0])
    prepare_range(8, 16)
    both((), NE_LATER[1])

    fth[...], ftl[...] = split(jnp.transpose(fg[2 * zh + a]))

    def product(t, s, h):
        near = jnp.where(t == 0, 0, jnp.where(t == 1, -2, jnp.where(t == 2, 2, 4)))
        odd = jnp.where(t == 0, -1, jnp.where(t == 1, 1, jnp.where(t == 2, -3, 3)))
        j = 2 * div(zz(jnp.where(eq, near, odd)), 2) + s
        base = pl.multiple_of(HALF * h, 8)
        keep = lax.broadcasted_iota(jnp.int32, (64, B), 0) < 60
        for k in range(4):
            value = fg[j, pl.ds(pl.multiple_of(base + 60 * k - 4 * (k % 2), 8), 64), :]
            if k % 2:
                value = pltpu.roll(value, 60, 0)
            high, rest = split(jnp.where(keep, value, 0.0))
            fph[64 * k : 64 * k + 64, :] = high
            fpl[64 * k : 64 * k + 64, :] = rest
        lanes = pl.ds(pl.multiple_of(256 * h, 256), 256)
        acc[...] += dot3((ah[j, :, lanes], al[j, :, lanes]), (fph[...], fpl[...]), ((1,), (0,)))

    def whole(t):
        for s in range(2):
            near = jnp.where(t == 0, 0, -2)
            odd = jnp.where(t == 0, -1, 1)
            j = 2 * div(zz(jnp.where(eq, near, odd)), 2) + s
            keep = lax.broadcasted_iota(jnp.int32, (64, B), 0) < 60
            for k in range(8):
                start = 60 * k - 4 * (k % 2)
                value = fg[j, start : start + 64, :]
                if k % 2:
                    value = pltpu.roll(value, 60, 0)
                high, rest = split(jnp.where(keep, value, 0.0))
                fwh[s, 64 * k : 64 * k + 64, :] = high
                fwl[s, 64 * k : 64 * k + 64, :] = rest
            acc[...] += dot3((ah[j], al[j]), (fwh[s], fwl[s]), ((1,), (0,)))

    def products(count, pick):
        def body(i, carry):
            product(*pick(i))
            return carry

        lax.fori_loop(0, count, body, 0)

    @pl.when(eq)
    def _():
        for q in range(NQ):
            f_wait(z, 1 - c, q)

    def last_wait(h):
        @pl.when(eq)
        def _():
            for q in range(h * NQ // 2, (h + 1) * NQ // 2):
                for s in range(2):
                    f_wait(zz(4), s, q)

    whole(0)
    both((), NE_LATER[2])
    whole(1)
    both((), NE_LATER[3])
    products(2, lambda i: (2, i, 0))
    last_wait(0)
    products(2, lambda i: (3, i, 0))
    both((), NE_LATER[4])
    products(2, lambda i: (2, i, 1))
    last_wait(1)
    products(2, lambda i: (3, i, 1))

    @pl.when(ne)
    def _():
        go(acc, cr, r_c.at[0], dev(x, y, 2 * zh + c, a), "ne")

    part[...] += dot3((fth[...], ftl[...]), split(acc[...]), ((1,), (0,)))

    @pl.when(ne)
    def _():
        go(part, pr, r_p.at[0], dev(x, y, zz(2 * a - 1), c), "ne")

    def give(k, core):
        owner = zz(2 * k)
        rows = pl.ds(pl.multiple_of(32 * (2 * div(owner, 2) + core), 32), 32)
        go(part.at[rows, :], dr.at[zh], r_d.at[zh], dev(x, y, owner, core), "eq")

    @pl.when(eq)
    def _():
        arrived(pr, r_p.at[0])
        part[...] += pr[...]
        for k in (2, 1, 3):
            give(k, c)
            give(k, 1 - c)
        give(0, 1 - c)

    @pl.when(eq)
    def _():
        dr[zh] = part[pl.ds(pl.multiple_of(32 * p, 32), 32), :]
        sel_v[...] = -masked(acc[...])

    @pl.when(ne)
    def _():
        arrived(cr, r_c.at[0])
        sel_v[...] = -masked(cr[...])

    sel_out = pltpu.make_async_copy(sel_v, sel_ref, local.at[0])
    sel_out.start()

    @pl.when(ne)
    def _():
        arrived(dr.at[zh], r_d.at[zh])

    for k in range(1, 4):
        arrived(dr.at[rem(zh + k, 4)], r_d.at[rem(zh + k, 4)])
    total = dr[0]
    for k in range(1, 4):
        total = total + dr[k]
    diag_v[...] = total
    diag_out = pltpu.make_async_copy(diag_v, diag_ref.at[0], local.at[1])
    diag_out.start()

    def finish(kind):
        like = {
            (CHUNK, B): fu.at[pl.ds(0, CHUNK), :],
            (U0, 128): ag0.at[0, 0, 0],
            (U1, 128): ag1.at[0, 0, 0],
            (1, U0, 128): ag0.at[0, 0, pl.ds(0, 1)],
            (3, U0, 128): ag0.at[0, 0, pl.ds(0, 3)],
            (B, B): part,
            (4, U0, 128): ag0.at[0, 0],
            (8, U1, 128): ag1.at[0, 0],
            (SLAB, B): acc,
            (32, B): lb.at[0],
        }
        for shape, index in pending[kind]:
            pltpu.make_async_remote_copy(
                src_ref=like[shape], dst_ref=like[shape], send_sem=send.at[index], recv_sem=r_l.at[0],
                device_id=sibling, device_id_type=MESH,
            ).wait_send()

    finish("all")

    @pl.when(eq)
    def _():
        finish("eq")

    @pl.when(ne)
    def _():
        finish("ne")

    sel_out.wait()
    diag_out.wait()


def hand_over(sel_ref, diag_ref, sel_out, diag_out):
    sel_out[...] = sel_ref[...]
    diag_out[...] = diag_ref[...]


def on_device(ancestor_inverse, factor, struct_rows, diag_factor_inverse):
    vmem = pl.BlockSpec(memory_space=pltpu.VMEM)
    anywhere = pl.BlockSpec(memory_space=pl.ANY)
    dma = pltpu.SemaphoreType.DMA
    shapes = (jax.ShapeDtypeStruct((SLAB, B), F32), jax.ShapeDtypeStruct((1, 32, B), F32))
    results = pl.pallas_call(
        kernel,
        out_shape=shapes,
        in_specs=[anywhere, anywhere, pl.BlockSpec(memory_space=pltpu.SMEM), anywhere],
        out_specs=(anywhere, anywhere),
        scratch_shapes=[
            pltpu.VMEM((SLAB, B), F32),
            pltpu.VMEM((32, B), F32),
            pltpu.VMEM((60, SLAB), F32),
            pltpu.VMEM((128, 512), F32),
            pltpu.VMEM((512, 128), F32),
            pltpu.VMEM((HALF, 128), F32),
            pltpu.VMEM((2, NY, NX, U0, 128), F32),
            pltpu.VMEM((2, NX, NY, U1, 128), F32),
            pltpu.VMEM((8, SLAB, 512), BF16),
            pltpu.VMEM((8, SLAB, 512), BF16),
            pltpu.VMEM((SLAB, B), F32),
            pltpu.VMEM((8, SLAB, B), F32),
            pltpu.VMEM((256, B), BF16),
            pltpu.VMEM((256, B), BF16),
            pltpu.VMEM((2, 512, B), BF16),
            pltpu.VMEM((2, 512, B), BF16),
            pltpu.VMEM((B, SLAB), BF16),
            pltpu.VMEM((B, SLAB), BF16),
            pltpu.VMEM((SLAB, B), F32),
            pltpu.VMEM((SLAB, B), F32),
            pltpu.VMEM((2, 32, B), F32),
            pltpu.VMEM((B, B), F32),
            pltpu.VMEM((B, B), F32),
            pltpu.VMEM((4, 32, B), F32),
            dma((3,)),
            dma((256,)),
            dma((2,)),
            dma((3,)),
            dma((8,)),
            dma((14,)),
            dma((24,)),
            dma((8,)),
            dma((4,)),
            dma((8 * NQ,)),
            dma((1,)),
            dma((1,)),
            dma((1,)),
            dma((4,)),
        ],
        compiler_params=pltpu.CompilerParams(
            collective_id=0, has_side_effects=True, vmem_limit_bytes=60 * 1024 * 1024
        ),
    )(ancestor_inverse.T, factor, struct_rows, diag_factor_inverse)
    return pl.pallas_call(
        hand_over,
        out_shape=shapes,
        in_specs=[vmem, vmem],
        out_specs=(vmem, vmem),
    )(*results)


def solution(mesh):
    placed = (P("pcol", "prow"), P("pcol", "prow"), P("prow", None), P("prow", "pcol", None))
    return jax.shard_map(
        on_device,
        mesh=mesh,
        in_specs=placed,
        out_specs=(P("pcol", "prow"), P("prow", "pcol", None)),
        check_vma=False,
    )
```
